512 devices in a mesh: dp: 64 (over z, x, y_lo), node: 8 (over y_hi, core).
Axes of the slice: x: 4, y: 8 (y_hi: 4, y_lo: 2; y = y_hi * 2 + y_lo), z: 8, core: 2. Of those that a mesh axis runs over, the one named last changes fastest.
Arguments:
- tokens: bfloat16 [1536, 5120], P('node'), may hold values from -6 to 6
- cotangent: bfloat16 [1536, 5120], P('node'), may hold values from -6 to 6
- gate_codes: bfloat16 [5120, 8192], P('node', 'dp'), may hold values from -16 to 16
- up_codes: bfloat16 [5120, 8192], P('node', 'dp'), may hold values from -16 to 16
- down_codes: bfloat16 [8192, 5120], P('dp', 'node'), may hold values from -4 to 4
- gate_scales: float32 [40, 8192], P(None, 'dp'), may hold values from 0.00559017 to 0.034938563
- up_scales: float32 [40, 8192], P(None, 'dp'), may hold values from 0.00559017 to 0.034938563
- down_scales: float32 [8192, 40], P('dp'), may hold values from 0.0044194176 to 0.027621359
Outputs:
- token_grad: bfloat16 [1536, 5120], P('node', 'dp')
- gate_grad: bfloat16 [5120, 8192], P('node', 'dp')
- up_grad: bfloat16 [5120, 8192], P('node', 'dp')
- down_grad: bfloat16 [8192, 5120], P('dp', 'node')
The draws below stay inside these ranges and needn't reach their ends.
All inputs are finite; a program needn't handle non-finite values.
Results may differ from the reference program's by a relative error of at most 0.0077.
Values may be sent and summed in bfloat16 or wider, within the bound.
A program may use at most 64 MiB of HBM per device.

```python
import math
import jax
import jax.numpy as jnp
from jax import lax

D = 5120
FF = 8192
QB = 128
TOK_DEV = 192
TOKENS = 1536
N_NODE = 8


def with_spikes(result, key, source, target, blocks, factor):
    owner, partner = [(jnp.arange(result.shape[dim]) // (result.shape[dim] // blocks)).reshape([-1 if axis == dim else 1 for axis in range(result.ndim)]) for dim in (source, target)]
    chosen = jax.random.permutation(key, blocks)[partner]
    strong = (owner == chosen) | (owner == (partner + blocks // 2) % blocks)
    return jnp.where(strong, factor * result, result)


def level_of(rng, dims, pieces, low, largest):
    level = 1.0
    for position, blocks in pieces:
        heights = jax.random.uniform(jax.random.fold_in(jax.random.fold_in(rng, 6), position), (blocks,), jnp.float32, low / len(pieces), largest / len(pieces))
        level = level * jnp.repeat(jnp.exp(heights), dims[position] // blocks).reshape((-1,) + (1,) * (len(dims) - 1 - position))
    return level


def scatter_about(stream_key, shape, spread, most, split=(), kind=jnp.bfloat16):
    array = jax.random.normal(stream_key, shape, jnp.float32) * spread
    if len(split) > 0:
        array = level_of(stream_key, shape, split, -0.22, 0.18) * array
    return jnp.clip(array, min=-most, max=most).astype(kind)


def bell_draw_with(key, extent, deviation, bound, pieces, heavy, kind=jnp.bfloat16):
    values = deviation * jax.random.normal(key, extent, jnp.float32)
    if pieces:
        values = values * level_of(key, extent, pieces, -0.22, 0.18)
    return jnp.clip(with_spikes(values, jax.random.fold_in(key, 3), *heavy), -bound, bound).astype(kind)


def setup_inputs(seed: int = 0) -> dict:
    streams_of = jax.random.split(jax.random.key(seed), 9)
    return {
        "tokens": bell_draw_with(streams_of[0], (TOKENS, D), 1.0, 6.0, ((0, 8),), (0, 1, 8, 2.0)),
        "cotangent": bell_draw_with(streams_of[1], (TOKENS, D), 1.0, 6.0, ((0, 8),), (0, 1, 8, 2.0)),
        "gate_codes": bell_draw_with(streams_of[2], (D, FF), 1.0, 16.0, ((0, 8), (1, 64)), (1, 0, 64, 4.0)),
        "up_codes": bell_draw_with(streams_of[3], (D, FF), 1.0, 16.0, ((0, 8), (1, 64)), (1, 0, 64, 4.0)),
        "down_codes": scatter_about(streams_of[4], (FF, D), 1.0, 4.0, ((0, 64), (1, 8))),
        "gate_scales": jnp.clip(jnp.exp(math.log(0.034938563) - 1.8325814 * jax.random.uniform(streams_of[5], (D // QB, FF), jnp.float32) ** level_of(streams_of[5], (D // QB, FF), ((1, 64),), -0.2, 0.2)), 0.00559017, 0.034938563),
        "up_scales": jnp.clip(jnp.exp(math.log(0.034938563) - 1.8325814 * jax.random.uniform(streams_of[6], (D // QB, FF), jnp.float32) ** level_of(streams_of[6], (D // QB, FF), ((1, 64),), -0.2, 0.2)), 0.00559017, 0.034938563),
        "down_scales": jnp.clip(jnp.exp(math.log(0.027621359) - 1.8325814 * jax.random.uniform(streams_of[7], (FF, D // QB), jnp.float32) ** level_of(streams_of[7], (FF, D // QB), ((0, 64),), -0.2, 0.2)), 0.0044194176, 0.027621359),
    }


def scale_rows(codes, scales):
    blocks = codes.astype(jnp.float32).reshape(scales.shape[0], QB, codes.shape[1])
    return (blocks * scales[:, None, :]).reshape(codes.shape).astype(jnp.bfloat16)


def contract(left, right):
    return lax.dot_general(left, right, (((0,), (0,)), ((), ())), preferred_element_type=jnp.float32)


def against(left, right):
    return lax.dot_general(left, right, (((1,), (1,)), ((), ())), preferred_element_type=jnp.float32)


def reference(tokens, cotangent, gate_codes, up_codes, down_codes, gate_scales, up_scales, down_scales):
    w_gate = scale_rows(gate_codes, gate_scales)
    w_up = scale_rows(up_codes, up_scales)
    w_down_t = scale_rows(down_codes.T, down_scales.T)
    gate = jnp.dot(tokens, w_gate, preferred_element_type=jnp.float32)
    upper = jnp.dot(tokens, w_up, preferred_element_type=jnp.float32)
    sig = jax.nn.sigmoid(gate)
    silu_val = gate * sig
    act = (silu_val * upper).astype(jnp.bfloat16)
    d_act = jnp.dot(cotangent, w_down_t, preferred_element_type=jnp.float32)
    d_gate = (d_act * upper * sig * (1.0 + gate * (1.0 - sig))).astype(jnp.bfloat16)
    d_up = (d_act * silu_val).astype(jnp.bfloat16)
    token_grad = (against(d_gate, w_gate) + against(d_up, w_up)).astype(jnp.bfloat16)
    tok_groups = tokens.reshape(N_NODE, TOK_DEV, D)
    cot_groups = cotangent.reshape(N_NODE, TOK_DEV, D)
    act_groups = act.reshape(N_NODE, TOK_DEV, FF)
    dg_groups = d_gate.reshape(N_NODE, TOK_DEV, FF)
    du_groups = d_up.reshape(N_NODE, TOK_DEV, FF)
    zero = jnp.zeros((D, FF), jnp.float32)

    def node_step(carry, items):
        rows, grad_rows, act_rows, dg_rows, du_rows = items
        parts = (contract(rows, dg_rows), contract(rows, du_rows), contract(grad_rows, act_rows))
        return tuple(c + p.astype(jnp.bfloat16).astype(jnp.float32) for c, p in zip(carry, parts)), None

    totals, unused = lax.scan(node_step, (zero, zero, zero), (tok_groups, cot_groups, act_groups, dg_groups, du_groups))
    gate_grad = totals[0].astype(jnp.bfloat16)
    up_grad = totals[1].astype(jnp.bfloat16)
    down_grad = totals[2].T.astype(jnp.bfloat16)
    return token_grad, gate_grad, up_grad, down_grad
```

```python
import jax
import jax.numpy as jnp
from jax import lax
from jax.experimental import pallas as pl
from jax.experimental.pallas import tpu as pltpu
from jax.sharding import PartitionSpec as P

BF = jnp.bfloat16
F32 = jnp.float32
MESH = pl.DeviceIdType.MESH

ROWS = 192
WIDE = 640
HID = 128
QB = 128
CUT = 48
N_COLS = 80


def dot_nn(a, b):
    return lax.dot_general(a, b, (((1,), (0,)), ((), ())), preferred_element_type=F32)


def dot_nt(a, b):
    return lax.dot_general(a, b, (((1,), (1,)), ((), ())), preferred_element_type=F32)


def dot_tn(a, b):
    return lax.dot_general(a, b, (((0,), (0,)), ((), ())), preferred_element_type=F32)


def kernel(
    tok, cot, gate_codes, up_codes, down_codes, gate_scales, up_scales, down_scales,
    token_grad, gate_grad, up_grad, down_grad,
    acts_in, w_gu, w_down, mine, other, mate_in, summed, terms_in,
    hidden, grad_out, down_out, grad_in, down_in, grad_own, down_own,
    up_buf, dn_buf, up_in, dn_in, last_buf, last_in,
    send_sems, recv_sems,
):
    dp = lax.axis_index("dp")
    node = lax.axis_index("node")
    z, x, low = dp // 8, (dp // 2) % 4, dp % 2
    chip, core = node // 2, node % 2
    par = x % 2
    mate = node + 1 - 2 * core
    pair = dp + 2 - 4 * par

    def at_z(step):
        return lax.rem(z + step + 8, 8) * 8 + x * 2 + low

    def at_chip(step):
        return lax.rem(chip + step + 4, 4)

    counts = {"send": 0, "recv": 0}

    def fresh(kind, number=1):
        first = counts[kind]
        counts[kind] += number
        return first

    sent = []

    def push(src, dst, recv, to_dp, to_node, when=None):
        copy = pltpu.make_async_remote_copy(
            src_ref=src, dst_ref=dst, send_sem=send_sems.at[fresh("send")], recv_sem=recv_sems.at[recv],
            device_id={"dp": to_dp, "node": to_node}, device_id_type=MESH,
        )
        if when is None:
            copy.start()
        else:
            pl.when(when)(copy.start)
        sent.append((copy, when))

    def landed(dst, recv):
        pltpu.make_async_copy(dst, dst, recv_sems.at[recv]).wait()

    barrier = pltpu.get_barrier_semaphore()

    def greet(to_dp, to_node):
        pl.semaphore_signal(barrier, inc=1, device_id={"dp": to_dp, "node": to_node}, device_id_type=MESH)

    for step in range(1, 8):
        greet(dp, lax.rem(node + step, 8))
    greet(at_z(1), node)
    greet(at_z(-1), node)
    greet(pair, node)
    loop_back = jnp.logical_and(z == node, par == core)
    for half in range(2):
        for hi in range(2):
            for lo in range(2):
                src_dp = (2 * chip + half) * 8 + (core + 2 * hi) * 2 + lo
                self_src = jnp.logical_and(src_dp == dp, z == node)
                pl.when(jnp.logical_not(self_src))(lambda a=src_dp: greet(a, z))

    for b in range(WIDE // QB):
        rows = slice(b * QB, (b + 1) * QB)
        line = pl.ds(node * (WIDE // QB) + b, 1)
        w_gu[0, rows, 0:HID] = (gate_codes[rows, :].astype(F32) * gate_scales[line, :]).astype(BF)
        w_gu[0, rows, HID:] = (up_codes[rows, :].astype(F32) * up_scales[line, :]).astype(BF)
        lanes = lax.broadcasted_iota(jnp.int32, down_scales.shape, 1)
        column = jnp.sum(
            jnp.where(lanes == node * (WIDE // QB) + b, down_scales[...], 0.0), axis=1, keepdims=True
        )
        w_down[0, :, rows] = (down_codes[:, rows].astype(F32) * column).astype(BF)

    pl.semaphore_wait(barrier, 18 - loop_back.astype(jnp.int32))

    is_src = core == par
    mine_cols = pl.ds(pl.multiple_of(node * WIDE, 128), WIDE)
    mate_cols = pl.ds(pl.multiple_of(mate * WIDE, 128), WIDE)
    fetch_recv = [fresh("recv") for _ in range(3)]
    own_recv = [fresh("recv") for _ in range(2)]
    own_rows = pl.ds(pl.multiple_of((z % 4) * CUT, 16), CUT)

    fetch_send = [[fresh("send") for _ in range(2)] for _ in range(3)]

    def fetch_copy(arr, a, step, kk):
        to_node = at_chip(step) * 2 + kk
        return pltpu.make_async_remote_copy(
            src_ref=arr.at[own_rows, pl.ds(pl.multiple_of(to_node * WIDE, 128), WIDE)],
            dst_ref=acts_in.at[a, chip, own_rows, :],
            send_sem=send_sems.at[fetch_send[step - 1][kk]], recv_sem=recv_sems.at[fetch_recv[step - 1]],
            device_id={"dp": dp, "node": to_node}, device_id_type=MESH,
        )

    for a, arr in enumerate((tok, cot)):
        @pl.when(jnp.logical_and(is_src, z // 4 == a))
        def _(a=a, arr=arr):
            for step in (2, 1, 3):
                for kk in range(2):
                    fetch_copy(arr, a, step, kk).start()

    w_recv = [fresh("recv") for _ in range(2)]
    push(w_gu.at[0], w_gu.at[1], w_recv[0], pair, node)
    push(w_down.at[0], w_down.at[1], w_recv[1], pair, node)

    own_copies = []
    for a, arr in enumerate((tok, cot)):
        push(arr.at[:, mate_cols], acts_in.at[a, chip], own_recv[a], dp, mate, when=is_src)

        @pl.when(is_src)
        def _(a=a, arr=arr):
            pltpu.make_async_copy(
                arr.at[:, mine_cols], acts_in.at[a, chip], recv_sems.at[own_recv[a]]
            ).start()

    up_recv = [[fresh("recv") for _ in range(3)] for _ in range(3)]
    dn_recv = [[fresh("recv") for _ in range(3)] for _ in range(3)]
    far_recv = [fresh("recv") for _ in range(3)]

    def block(turn, step):
        piece = lax.rem(z + turn + 8, 8)
        return acts_in.at[
            piece // 4, at_chip(-step), pl.ds(pl.multiple_of((piece % 4) * CUT, 16), CUT), :
        ]

    def relay(turn):
        for step in (1, 3, 2):
            if turn == 0:
                landed(block(0, step), fetch_recv[step - 1])
                push(block(0, step), block(0, step), up_recv[0][step - 1], at_z(1), node)
                push(block(0, step), block(0, step), dn_recv[0][step - 1], at_z(-1), node)
                continue
            if turn == 4:
                landed(block(4, step), far_recv[step - 1])
                continue
            here = block(-turn, step)
            landed(here, up_recv[turn - 1][step - 1])
            if turn < 3:
                push(here, here, up_recv[turn][step - 1], at_z(1), node)
            elif step != 3:
                push(here, here, far_recv[step - 1], at_z(1), node, when=None if step == 1 else core == 0)
            here = block(turn, step)
            landed(here, dn_recv[turn - 1][step - 1])
            if turn < 3:
                push(here, here, dn_recv[turn][step - 1], at_z(-1), node)
            elif step != 1:
                push(here, here, far_recv[step - 1], at_z(-1), node, when=None if step == 3 else core == 1)

    mate_recv = [fresh("recv") for _ in range(8)]
    mate_send = [fresh("send") for _ in range(8)]
    term_recv = [[fresh("recv") for _ in range(3)] for _ in range(8)]
    term_send = [[fresh("send") for _ in range(3)] for _ in range(8)]
    spans = (slice(0, 2 * HID), slice(2 * HID, 3 * HID))

    def place(turn):
        piece = lax.rem(z + turn + 8, 8)
        return piece // 4, pl.ds(pl.multiple_of((piece % 4) * CUT, 16), CUT)

    def mate_copy(turn, a, rows):
        return pltpu.make_async_remote_copy(
            src_ref=other.at[:, rows, spans[a]], dst_ref=mate_in.at[:, rows, spans[a]],
            send_sem=send_sems.at[mate_send[turn]], recv_sem=recv_sems.at[mate_recv[turn]],
            device_id={"dp": dp, "node": mate}, device_id_type=MESH,
        )

    def term_copy(turn, a, rows, step):
        return pltpu.make_async_remote_copy(
            src_ref=summed.at[at_chip(step), rows, spans[a]], dst_ref=terms_in.at[step - 1, rows, spans[a]],
            send_sem=send_sems.at[term_send[turn][step - 1]], recv_sem=recv_sems.at[term_recv[turn][step - 1]],
            device_id={"dp": dp, "node": at_chip(step) * 2 + core}, device_id_type=MESH,
        )

    def multiply(turn):
        which, rows = place(turn)
        for a in range(2):
            @pl.when(which == a)
            def _(a=a):
                data = acts_in[a, :, rows, :].reshape(4 * CUT, WIDE)
                for part, store in ((1 - core, other), (core, mine)):
                    if a == 0:
                        out = dot_nn(data, w_gu[part])
                    else:
                        out = dot_nt(data, w_down[part])
                    store[:, rows, spans[a]] = out.reshape(4, CUT, -1).astype(store.dtype)
                    if store is other:
                        mate_copy(turn % 8, a, rows).start()

    def combine(turn):
        which, rows = place(turn)
        for a in range(2):
            @pl.when(which == a)
            def _(a=a):
                mate_copy(turn % 8, a, rows).wait_recv()
                total = mine[:, rows, spans[a]] + mate_in[:, rows, spans[a]].astype(F32)
                mine[:, rows, spans[a]] = total
                summed[:, rows, spans[a]] = total.astype(BF)
                for step in (2, 1, 3):
                    term_copy(turn % 8, a, rows, step).start()

    def collect(turn):
        which, rows = place(turn)
        for a in range(2):
            @pl.when(which == a)
            def _(a=a):
                for step in range(1, 4):
                    term_copy(turn % 8, a, rows, step).wait_recv()

    relay(0)
    for a in range(2):
        landed(acts_in.at[a, chip], own_recv[a])
    relay(1)
    landed(w_gu.at[1], w_recv[0])
    landed(w_down.at[1], w_recv[1])
    multiply(0)
    relay(2)
    multiply(-1)
    combine(0)
    multiply(1)
    combine(-1)
    relay(3)
    multiply(-2)
    combine(1)
    multiply(2)
    combine(-2)
    multiply(-3)
    combine(2)
    multiply(3)
    combine(-3)
    relay(4)
    multiply(4)
    combine(3)
    combine(4)
    for turn in range(8):
        collect(turn)

    full = mine[chip]
    for step in range(3):
        full = full + terms_in[step].astype(F32)
    gate, upper, d_act = full[:, 0:HID], full[:, HID : 2 * HID], full[:, 2 * HID :]
    sig = jax.nn.sigmoid(gate)
    silu = gate * sig
    hidden[core, chip, :, 0:HID] = (d_act * upper * sig * (1.0 + gate * (1.0 - sig))).astype(BF)
    hidden[core, chip, :, HID : 2 * HID] = (d_act * silu).astype(BF)
    hidden[core, chip, :, 2 * HID :] = (silu * upper).astype(BF)

    hid_recv = [fresh("recv") for _ in range(3)]
    hid_mate = [fresh("recv") for _ in range(4)]
    own_hid = hidden.at[core, chip]
    for step in (2, 1, 3):
        push(own_hid, own_hid, hid_recv[step - 1], dp, at_chip(step) * 2 + core)
    push(own_hid, own_hid, hid_mate[0], dp, mate)
    for step in (1, 3, 2):
        here = hidden.at[core, at_chip(-step)]
        landed(here, hid_recv[step - 1])
        push(here, here, hid_mate[step], dp, mate)
    for step in range(4):
        landed(hidden.at[1 - core, at_chip(-step)], hid_mate[step])

    def weight_grads(part):
        tokens = acts_in[0].reshape(4 * ROWS, WIDE)
        grads = acts_in[1].reshape(4 * ROWS, WIDE)
        back = hidden[part].reshape(4 * ROWS, 3 * HID)
        return dot_tn(tokens, back[:, 0 : 2 * HID]), dot_tn(back[:, 2 * HID :], grads)

    first, second = weight_grads(1)
    grad_out[...] = first.astype(BF)
    down_out[...] = second.astype(BF)
    grad_recv = [fresh("recv") for _ in range(2)]
    push(grad_out, grad_in, grad_recv[0], pair, node)
    push(down_out, down_in, grad_recv[1], pair, node)

    def token_terms(turn):
        piece = lax.rem(z + turn + 8, 8)
        rows = pl.ds(pl.multiple_of((piece % 2) * 96, 16), 96)
        return sum(
            dot_nt(hidden[part, piece // 2, rows, 0 : 2 * HID], w_gu[part]) for part in range(2)
        )

    ring = {}
    for way in (1, -1):
        for far in range(1, 5):
            for cut in range(2):
                if far == 4 and cut != (0 if way == 1 else 1):
                    continue
                ring[way, far, cut] = fresh("recv")

    def cut_rows(cut):
        return slice(cut * CUT, (cut + 1) * CUT)

    def ring_step(way, far, terms):
        buf, into = (up_buf, up_in) if way == 1 else (dn_buf, dn_in)
        for cut in range(2):
            if (way, far, cut) not in ring:
                continue
            rows = cut_rows(cut)
            value = terms[rows]
            if (way, far + 1, cut) in ring:
                landed(into.at[far, rows], ring[way, far + 1, cut])
                value = value + into[far, rows].astype(F32)
            buf[far - 1, rows] = value.astype(BF)
            push(buf.at[far - 1, rows], into.at[far - 1, rows], ring[way, far, cut], at_z(way), node)

    terms = token_terms(4)
    ring_step(1, 4, terms)
    ring_step(-1, 4, terms)
    for far in (3, 2, 1):
        ahead = token_terms(far)
        behind = token_terms(-far)
        ring_step(1, far, ahead)
        ring_step(-1, far, behind)
    terms = token_terms(0)

    first, second = weight_grads(0)
    grad_own[...] = first
    down_own[...] = second

    for way, into in ((1, up_in), (-1, dn_in)):
        for cut in range(2):
            landed(into.at[0, cut_rows(cut)], ring[way, 1, cut])
    terms = terms + up_in[0].astype(F32) + dn_in[0].astype(F32)
    for i in range(8):
        last_buf[i, :, 0:N_COLS] = terms[:, i * N_COLS : (i + 1) * N_COLS].astype(BF)
        last_buf[i, :, N_COLS:] = jnp.zeros((96, 128 - N_COLS), BF)

    last_recv = fresh("recv", 8)
    slot = (z % 2) * 4 + (x // 2) * 2 + low
    last_node = 2 * (z // 2) + par
    for i in range(8):
        to_dp = node * 8 + i
        to_self = jnp.logical_and(to_dp == dp, last_node == node)
        push(last_buf.at[i], last_in.at[slot], last_recv + slot, to_dp, last_node, when=jnp.logical_not(to_self))

        @pl.when(to_self)
        def _(i=i):
            pltpu.make_async_copy(last_buf.at[i], last_in.at[slot], recv_sems.at[last_recv + slot]).start()

    landed(grad_in, grad_recv[0])
    landed(down_in, grad_recv[1])
    gate_grad[...] = (grad_own[:, 0:HID] + grad_in[:, 0:HID].astype(F32)).astype(BF)
    up_grad[...] = (grad_own[:, HID:] + grad_in[:, HID:].astype(F32)).astype(BF)
    down_grad[...] = (down_own[...] + down_in[...].astype(F32)).astype(BF)

    for i in range(8):
        landed(last_in.at[i], last_recv + i)
    for half in range(2):
        total = last_in[4 * half].astype(F32)
        for i in range(1, 4):
            total = total + last_in[4 * half + i].astype(F32)
        token_grad[half * 96 : (half + 1) * 96, :] = total[:, 0:N_COLS].astype(BF)

    for copy, when in sent:
        if when is None:
            copy.wait_send()
        else:
            pl.when(when)(copy.wait_send)
    for a, arr in enumerate((tok, cot)):
        @pl.when(jnp.logical_and(is_src, z // 4 == a))
        def _(a=a, arr=arr):
            for step in range(1, 4):
                for kk in range(2):
                    fetch_copy(arr, a, step, kk).wait_send()
    for turn in range(8):
        which, rows = place(turn)
        for a in range(2):
            @pl.when(which == a)
            def _(a=a, turn=turn, rows=rows):
                mate_copy(turn, a, rows).wait_send()
                for step in range(1, 4):
                    term_copy(turn, a, rows, step).wait_send()


def body(*args):
    vmem = pl.BlockSpec(memory_space=pltpu.VMEM)
    hbm = pl.BlockSpec(memory_space=pl.ANY)
    return pl.pallas_call(
        kernel,
        out_shape=(
            jax.ShapeDtypeStruct((ROWS, N_COLS), BF),
            jax.ShapeDtypeStruct((WIDE, HID), BF),
            jax.ShapeDtypeStruct((WIDE, HID), BF),
            jax.ShapeDtypeStruct((HID, WIDE), BF),
        ),
        in_specs=[hbm, hbm] + [vmem] * 6,
        out_specs=(vmem,) * 4,
        scratch_shapes=[
            pltpu.VMEM((2, 4, ROWS, WIDE), BF),
            pltpu.VMEM((2, WIDE, 2 * HID), BF),
            pltpu.VMEM((2, HID, WIDE), BF),
            pltpu.VMEM((4, ROWS, 3 * HID), F32),
            pltpu.VMEM((4, ROWS, 3 * HID), BF),
            pltpu.VMEM((4, ROWS, 3 * HID), BF),
            pltpu.VMEM((4, ROWS, 3 * HID), BF),
            pltpu.VMEM((3, ROWS, 3 * HID), BF),
            pltpu.VMEM((2, 4, ROWS, 3 * HID), BF),
            pltpu.VMEM((WIDE, 2 * HID), BF),
            pltpu.VMEM((HID, WIDE), BF),
            pltpu.VMEM((WIDE, 2 * HID), BF),
            pltpu.VMEM((HID, WIDE), BF),
            pltpu.VMEM((WIDE, 2 * HID), F32),
            pltpu.VMEM((HID, WIDE), F32),
            pltpu.VMEM((4, 96, WIDE), BF),
            pltpu.VMEM((4, 96, WIDE), BF),
            pltpu.VMEM((4, 96, WIDE), BF),
            pltpu.VMEM((4, 96, WIDE), BF),
            pltpu.VMEM((8, 96, 128), BF),
            pltpu.VMEM((8, 96, 128), BF),
            pltpu.SemaphoreType.DMA((112,)),
            pltpu.SemaphoreType.DMA((112,)),
        ],
        compiler_params=pltpu.CompilerParams(
            collective_id=0, has_side_effects=True, vmem_limit_bytes=48 * 1024 * 1024
        ),
        cost_estimate=pl.CostEstimate(flops=2_100_000_000, bytes_accessed=5_000_000, transcendentals=25_000),
    )(*args)


def solution(mesh):
    return jax.shard_map(
        body,
        mesh=mesh,
        in_specs=(
            P("node", None),
            P("node", None),
            P("node", "dp"),
            P("node", "dp"),
            P("dp", "node"),
            P(None, "dp"),
            P(None, "dp"),
            P("dp", None),
        ),
        out_specs=(P("node", "dp"), P("node", "dp"), P("node", "dp"), P("dp", "node")),
        check_vma=False,
    )
```

```python
import jax
import jax.numpy as jnp
from jax import lax
from jax.experimental import pallas as pl
from jax.experimental.pallas import tpu as pltpu
from jax.sharding import PartitionSpec as P

BF = jnp.bfloat16
F32 = jnp.float32
MESH = pl.DeviceIdType.MESH

ROWS = 192
WIDE = 640
HID = 128
QB = 128
CUT = 48
VMEM_BYTES = 60 * 1024 * 1024
N_COLS = 80


def dot_nn(a, b):
    return lax.dot_general(a, b, (((1,), (0,)), ((), ())), preferred_element_type=F32)


def dot_nt(a, b):
    return lax.dot_general(a, b, (((1,), (1,)), ((), ())), preferred_element_type=F32)


def dot_tn(a, b):
    return lax.dot_general(a, b, (((0,), (0,)), ((), ())), preferred_element_type=F32)


def kernel(
    tok, cot, gate_codes_hbm, up_codes_hbm, down_codes_hbm, gate_scales_hbm, up_scales_hbm, down_scales_hbm,
    token_grad_hbm, gate_grad_hbm, up_grad_hbm, down_grad_hbm,
    token_grad, gate_grad, up_grad, down_grad, gate_codes, up_codes, down_codes, gate_scales, up_scales, down_scales,
    acts_in, fetch_relay, w_gu, w_down, mine, other, mate_in, far_out, far_in, near_out, near_in,
    hidden, grad_out, down_out, grad_in, down_in, grad_own, down_own,
    up_buf, dn_buf, up_in, dn_in, side_buf, side_in, last_buf, last_in,
    load_sems, store_sems, send_sems, recv_sems,
):
    dp = lax.axis_index("dp")
    node = lax.axis_index("node")
    z, x, low = dp // 8, (dp // 2) % 4, dp % 2
    chip, core = node // 2, node % 2
    par = x % 2
    mate = node + 1 - 2 * core
    pair = dp + 2 - 4 * par
    toward = 1 - 2 * core
    side = (x // 2) * 2 + low

    def at_z(step):
        return lax.rem(z + step + 8, 8) * 8 + x * 2 + low

    def at_chip(step):
        return lax.rem(chip + step + 4, 4)

    def at_side(member):
        return z * 8 + (par + 2 * (member // 2)) * 2 + member % 2

    loads = [
        pltpu.make_async_copy(src, dst, load_sems.at[i])
        for i, (src, dst) in enumerate((
            (gate_codes_hbm, gate_codes), (up_codes_hbm, up_codes), (down_codes_hbm, down_codes),
            (gate_scales_hbm, gate_scales), (up_scales_hbm, up_scales), (down_scales_hbm, down_scales),
        ))
    ]
    for load in loads:
        load.start()

    counts = {"send": 0, "recv": 0}

    def fresh(kind, number=1):
        first = counts[kind]
        counts[kind] += number
        return first

    sent = []

    def push(src, dst, recv, to_dp, to_node, when=None):
        copy = pltpu.make_async_remote_copy(
            src_ref=src, dst_ref=dst, send_sem=send_sems.at[fresh("send")], recv_sem=recv_sems.at[recv],
            device_id={"dp": to_dp, "node": to_node}, device_id_type=MESH,
        )
        if when is None:
            copy.start()
        else:
            pl.when(when)(copy.start)
        sent.append((copy, when))

    def landed(dst, recv):
        pltpu.make_async_copy(dst, dst, recv_sems.at[recv]).wait()

    barrier = pltpu.get_barrier_semaphore()

    def greet(to_dp, to_node):
        pl.semaphore_signal(barrier, inc=1, device_id={"dp": to_dp, "node": to_node}, device_id_type=MESH)

    for step in range(1, 8):
        greet(dp, lax.rem(node + step, 8))
    greet(at_z(1), node)
    greet(at_z(-1), node)
    greet(pair, node)
    for step in range(1, 4):
        greet(at_side(lax.rem(side + step, 4)), node)
    loop_back = jnp.logical_and(jnp.logical_and(z == node, par == core), low == par)
    for half in range(2):
        src_dp = (2 * chip + half) * 8 + (core + 2 * (x // 2)) * 2 + par
        self_src = jnp.logical_and(src_dp == dp, z == node)
        pl.when(jnp.logical_not(self_src))(lambda a=src_dp: greet(a, z))

    for load in loads:
        load.wait()
    eye = lax.broadcasted_iota(jnp.int32, (HID, HID), 0) == lax.broadcasted_iota(jnp.int32, (HID, HID), 1)
    for b in range(WIDE // QB):
        rows = slice(b * QB, (b + 1) * QB)
        line = pl.ds(node * (WIDE // QB) + b, 1)
        w_gu[0, rows, 0:HID] = (gate_codes[rows, :].astype(F32) * gate_scales[line, :]).astype(BF)
        w_gu[0, rows, HID:] = (up_codes[rows, :].astype(F32) * up_scales[line, :]).astype(BF)
        column = jnp.sum(jnp.where(eye, down_scales[line, :], 0.0), axis=1, keepdims=True)
        w_down[0, :, rows] = (down_codes[:, rows].astype(F32) * column).astype(BF)

    pl.semaphore_wait(barrier, 15 - loop_back.astype(jnp.int32))

    def quarter_rows(quarter):
        return pl.ds(pl.multiple_of(quarter * CUT, 16), CUT)

    def cols_of(to_node):
        return pl.ds(pl.multiple_of(to_node * WIDE, 128), WIDE)

    is_src = core == par
    fetch_recv = [fresh("recv") for _ in range(3)]
    relay_recv = fresh("recv")
    own_recv = [fresh("recv") for _ in range(2)]
    fetch_send = [[fresh("send") for _ in range(2)] for _ in range(3)]
    own_rows = quarter_rows(z // 2)

    def fetch_copy(arr, a, step, kk):
        owner = at_chip(step) * 2 + kk
        if step == 2:
            dst, to_node, recv = fetch_relay, at_chip(1 - 2 * kk) * 2 + kk, relay_recv
        else:
            dst, to_node, recv = acts_in.at[a, chip, own_rows, :], owner, fetch_recv[step - 1]
        return pltpu.make_async_remote_copy(
            src_ref=arr.at[own_rows, cols_of(owner)], dst_ref=dst,
            send_sem=send_sems.at[fetch_send[step - 1][kk]], recv_sem=recv_sems.at[recv],
            device_id={"dp": dp, "node": to_node}, device_id_type=MESH,
        )

    for a, arr in enumerate((tok, cot)):
        @pl.when(jnp.logical_and(is_src, z % 2 == a))
        def _(a=a, arr=arr):
            for step in (2, 1, 3):
                for kk in range(2):
                    fetch_copy(arr, a, step, kk).start()

    w_recv = [fresh("recv") for _ in range(2)]
    push(w_gu.at[0], w_gu.at[1], w_recv[0], pair, node)
    push(w_down.at[0], w_down.at[1], w_recv[1], pair, node)

    for a, arr in enumerate((tok, cot)):
        push(arr.at[:, cols_of(mate)], acts_in.at[a, chip], own_recv[a], dp, mate, when=is_src)

        @pl.when(is_src)
        def _(a=a, arr=arr):
            pltpu.make_async_copy(
                arr.at[:, cols_of(node)], acts_in.at[a, chip], recv_sems.at[own_recv[a]]
            ).start()

    up_recv = [[fresh("recv") for _ in range(3)] for _ in range(3)]
    dn_recv = [[fresh("recv") for _ in range(3)] for _ in range(3)]
    far_recv = [fresh("recv") for _ in range(3)]

    def block(turn, step):
        piece = lax.rem(z + turn + 8, 8)
        return acts_in.at[piece % 2, at_chip(-step), quarter_rows(piece // 2), :]

    def relay(turn, step):
        if turn == 0:
            landed(block(0, step), fetch_recv[step - 1])
            push(block(0, step), block(0, step), up_recv[0][step - 1], at_z(1), node)
            push(block(0, step), block(0, step), dn_recv[0][step - 1], at_z(-1), node)
            return
        if turn == 4:
            landed(block(4, step), far_recv[step - 1])
            return
        here = block(-turn, step)
        landed(here, up_recv[turn - 1][step - 1])
        if turn < 3:
            push(here, here, up_recv[turn][step - 1], at_z(1), node)
        elif step != 3:
            push(here, here, far_recv[step - 1], at_z(1), node, when=None if step == 1 else core == 0)
        here = block(turn, step)
        landed(here, dn_recv[turn - 1][step - 1])
        if turn < 3:
            push(here, here, dn_recv[turn][step - 1], at_z(-1), node)
        elif step != 1:
            push(here, here, far_recv[step - 1], at_z(-1), node, when=None if step == 3 else core == 1)

    sign = 1 - 2 * (z % 2)
    quarters = [
        lax.rem(z + first * sign + 8, 8) // 2 for first in (0, -1, 2, -3)
    ]
    mate_recv = [fresh("recv") for _ in range(4)]
    relay_sum_recv = [[fresh("recv") for _ in range(3)] for _ in range(4)]
    near_recv = [[fresh("recv") for _ in range(2)] for _ in range(4)]
    hid_near = [[fresh("recv") for _ in range(2)] for _ in range(4)]
    hid_far = [[fresh("recv") for _ in range(3)] for _ in range(4)]
    hid_mate = [[fresh("recv") for _ in range(4)] for _ in range(4)]
    near_steps = (1, -1)
    ways = (1, toward, -1)
    lane = lax.broadcasted_iota(jnp.int32, (CUT, 3 * HID), 1)
    goes_up = lane < 2 * HID - core * HID

    def cols(b):
        return slice(b * HID, (b + 1) * HID)

    def multiply(s):
        rows = quarter_rows(quarters[s])
        tokens = acts_in[0, :, rows, :].reshape(4 * CUT, WIDE)
        grads = acts_in[1, :, rows, :].reshape(4 * CUT, WIDE)
        for part, store in ((1 - core, other), (core, mine)):
            store[s, :, :, 0 : 2 * HID] = (
                dot_nn(tokens, w_gu[part]).reshape(4, CUT, 2 * HID).astype(store.dtype)
            )
            store[s, :, :, 2 * HID :] = (
                dot_nt(grads, w_down[part]).reshape(4, CUT, HID).astype(store.dtype)
            )
            if store is other:
                push(other.at[s], mate_in.at[s], mate_recv[s], dp, mate)

    def combine(s):
        landed(mate_in.at[s], mate_recv[s])
        opposite = at_chip(2)
        far_out[s] = (mine[s, opposite] + mate_in[s, opposite].astype(F32)).astype(BF)
        for b in range(3):
            push(
                far_out.at[s, :, cols(b)], far_in.at[s, :, cols(b)], relay_sum_recv[s][b],
                dp, at_chip(ways[b]) * 2 + core,
            )

    def forward_sum(s):
        for b in range(3):
            landed(far_in.at[s, :, cols(b)], relay_sum_recv[s][b])
        passing = far_in[s].astype(F32)
        for i, step in enumerate(near_steps):
            to = at_chip(step)
            extra = jnp.where(goes_up, passing, 0.0) if step == 1 else jnp.where(goes_up, 0.0, passing)
            near_out[s, i] = (mine[s, to] + mate_in[s, to].astype(F32) + extra).astype(BF)
            push(near_out.at[s, i], near_in.at[s, i], near_recv[s][i], dp, to * 2 + core)

    def activate(s):
        full = mine[s, chip] + mate_in[s, chip].astype(F32)
        for i in range(2):
            landed(near_in.at[s, i], near_recv[s][i])
            full = full + near_in[s, i].astype(F32)
        rows = quarter_rows(quarters[s])
        gate, upper, d_act = full[:, 0:HID], full[:, HID : 2 * HID], full[:, 2 * HID :]
        sig = jax.nn.sigmoid(gate)
        silu = gate * sig
        hidden[core, chip, rows, 0:HID] = (d_act * upper * sig * (1.0 + gate * (1.0 - sig))).astype(BF)
        hidden[core, chip, rows, HID : 2 * HID] = (d_act * silu).astype(BF)
        hidden[core, chip, rows, 2 * HID :] = (silu * upper).astype(BF)
        own = hidden.at[core, chip, rows]
        for i, step in enumerate(near_steps):
            push(own, own, hid_near[s][i], dp, at_chip(step) * 2 + core)
        push(own, own, hid_mate[s][0], dp, mate)

    def forward_hidden(s):
        rows = quarter_rows(quarters[s])
        for i, step in enumerate(near_steps):
            landed(hidden.at[core, at_chip(-step), rows], hid_near[s][i])
        for b in range(3):
            here = hidden.at[core, at_chip(-ways[b]), rows, cols(b)]
            push(here, here, hid_far[s][b], dp, at_chip(ways[b]) * 2 + core)
        for i, step in enumerate(near_steps):
            here = hidden.at[core, at_chip(-step), rows]
            push(here, here, hid_mate[s][1 + i], dp, mate)

    def last_hidden(s):
        rows = quarter_rows(quarters[s])
        for b in range(3):
            landed(hidden.at[core, at_chip(2), rows, cols(b)], hid_far[s][b])
        here = hidden.at[core, at_chip(2), rows]
        push(here, here, hid_mate[s][3], dp, mate)

    def finish_hidden(s):
        rows = quarter_rows(quarters[s])
        for i, step in enumerate((0, -1, 1, 2)):
            landed(hidden.at[1 - core, at_chip(step), rows], hid_mate[s][i])

    landed(fetch_relay, relay_recv)
    passed = acts_in.at[z % 2, at_chip(-toward), own_rows, :]
    push(fetch_relay, passed, fetch_recv[1], dp, at_chip(toward) * 2 + core)
    relay(0, 1)
    relay(0, 3)
    relay(0, 2)
    relay(1, 1)
    relay(1, 3)
    for a in range(2):
        landed(acts_in.at[a, chip], own_recv[a])
    relay(1, 2)
    landed(w_gu.at[1], w_recv[0])
    landed(w_down.at[1], w_recv[1])
    multiply(0)
    relay(2, 1)
    combine(0)
    relay(2, 3)
    relay(2, 2)
    multiply(1)
    forward_sum(0)
    relay(3, 1)
    combine(1)
    activate(0)
    relay(3, 3)
    relay(3, 2)
    multiply(2)
    forward_sum(1)
    forward_hidden(0)
    relay(4, 1)
    combine(2)
    activate(1)
    relay(4, 3)
    relay(4, 2)
    multiply(3)
    forward_sum(2)
    last_hidden(0)
    forward_hidden(1)
    combine(3)
    activate(2)
    last_hidden(1)
    forward_sum(3)
    forward_hidden(2)
    activate(3)
    last_hidden(2)
    forward_hidden(3)
    last_hidden(3)
    for s in range(4):
        finish_hidden(s)

    def token_terms(turn):
        piece = lax.rem(z + turn + 8, 8)
        rows = pl.ds(pl.multiple_of((piece % 2) * 96, 16), 96)
        return sum(
            dot_nt(hidden[part, piece // 2, rows, 0 : 2 * HID], w_gu[part]) for part in range(2)
        )

    ring = {}
    for way in (1, -1):
        for far in range(1, 5):
            for cut in range(2):
                if far == 4 and cut != (0 if way == 1 else 1):
                    continue
                ring[way, far, cut] = fresh("recv")

    def cut_rows(cut):
        return slice(cut * CUT, (cut + 1) * CUT)

    def ring_step(way, far, terms):
        buf, into = (up_buf, up_in) if way == 1 else (dn_buf, dn_in)
        for cut in range(2):
            if (way, far, cut) not in ring:
                continue
            rows = cut_rows(cut)
            value = terms[rows]
            if (way, far + 1, cut) in ring:
                landed(into.at[far, rows], ring[way, far + 1, cut])
                value = value + into[far, rows].astype(F32)
            buf[far - 1, rows] = value.astype(BF)
            push(buf.at[far - 1, rows], into.at[far - 1, rows], ring[way, far, cut], at_z(way), node)

    def weight_grads(part):
        tokens = acts_in[0].reshape(4 * ROWS, WIDE)
        grads = acts_in[1].reshape(4 * ROWS, WIDE)
        back = hidden[part].reshape(4 * ROWS, 3 * HID)
        return dot_tn(tokens, back[:, 0 : 2 * HID]), dot_tn(back[:, 2 * HID :], grads)

    terms = token_terms(4)
    ring_step(1, 4, terms)
    ring_step(-1, 4, terms)

    first, second = weight_grads(1)
    grad_out[...] = first.astype(BF)
    down_out[...] = second.astype(BF)
    grad_recv = [fresh("recv") for _ in range(2)]
    push(grad_out, grad_in, grad_recv[0], pair, node)
    push(down_out, down_in, grad_recv[1], pair, node)

    for far in (3, 2, 1):
        ahead = token_terms(far)
        behind = token_terms(-far)
        ring_step(1, far, ahead)
        ring_step(-1, far, behind)
    terms = token_terms(0)

    first, second = weight_grads(0)
    grad_own[...] = first
    down_own[...] = second

    for way, into in ((1, up_in), (-1, dn_in)):
        for cut in range(2):
            landed(into.at[0, cut_rows(cut)], ring[way, 1, cut])
    terms = terms + up_in[0].astype(F32) + dn_in[0].astype(F32)
    for i in range(8):
        side_buf[i // 2, i % 2, :, 0:N_COLS] = terms[:, i * N_COLS : (i + 1) * N_COLS].astype(BF)
        side_buf[i // 2, i % 2, :, N_COLS:] = jnp.zeros((96, 128 - N_COLS), BF)

    side_recv = [fresh("recv") for _ in range(3)]
    for step in range(1, 4):
        to = lax.rem(side + step, 4)
        push(side_buf.at[to], side_in.at[step - 1], side_recv[step - 1], at_side(to), node)
    total = side_buf[side].astype(F32)
    for step in range(1, 4):
        landed(side_in.at[step - 1], side_recv[step - 1])
        total = total + side_in[step - 1].astype(F32)
    last_buf[...] = total.astype(BF)

    last_recv = fresh("recv", 2)
    slot = z % 2
    last_node = 2 * (z // 2) + par
    for i in range(2):
        to_dp = node * 8 + side * 2 + i
        to_self = jnp.logical_and(to_dp == dp, last_node == node)
        push(last_buf.at[i], last_in.at[slot], last_recv + slot, to_dp, last_node, when=jnp.logical_not(to_self))

        @pl.when(to_self)
        def _(i=i):
            pltpu.make_async_copy(last_buf.at[i], last_in.at[slot], recv_sems.at[last_recv + slot]).start()

    landed(grad_in, grad_recv[0])
    landed(down_in, grad_recv[1])
    gate_grad[...] = (grad_own[:, 0:HID] + grad_in[:, 0:HID].astype(F32)).astype(BF)
    up_grad[...] = (grad_own[:, HID:] + grad_in[:, HID:].astype(F32)).astype(BF)
    down_grad[...] = (down_own[...] + down_in[...].astype(F32)).astype(BF)
    stores = [
        pltpu.make_async_copy(src, dst, store_sems.at[i])
        for i, (src, dst) in enumerate((
            (gate_grad, gate_grad_hbm), (up_grad, up_grad_hbm), (down_grad, down_grad_hbm),
            (token_grad, token_grad_hbm),
        ))
    ]
    for store in stores[:3]:
        store.start()

    for i in range(2):
        landed(last_in.at[i], last_recv + i)
    token_grad[...] = jnp.transpose(last_in[...].reshape(ROWS, 128).astype(F32))[0:N_COLS, :].astype(BF)
    stores[3].start()

    for copy, when in sent:
        if when is None:
            copy.wait_send()
        else:
            pl.when(when)(copy.wait_send)
    for a, arr in enumerate((tok, cot)):
        @pl.when(jnp.logical_and(is_src, z % 2 == a))
        def _(a=a, arr=arr):
            for step in range(1, 4):
                for kk in range(2):
                    fetch_copy(arr, a, step, kk).wait_send()
    for store in stores:
        store.wait()


def write_out(*refs):
    copies = [
        pltpu.make_async_copy(refs[i], refs[4 + i], refs[8].at[i]) for i in range(4)
    ]
    for copy in copies:
        copy.start()
    for copy in copies:
        copy.wait()


def body(tok, cot, gate_codes, up_codes, down_codes, gate_scales, up_scales, down_scales):
    hbm = pl.BlockSpec(memory_space=pltpu.HBM)
    outs = (
        jax.ShapeDtypeStruct((N_COLS, ROWS), BF),
        jax.ShapeDtypeStruct((WIDE, HID), BF),
        jax.ShapeDtypeStruct((WIDE, HID), BF),
        jax.ShapeDtypeStruct((HID, WIDE), BF),
    )
    results = pl.pallas_call(
        kernel,
        out_shape=outs,
        in_specs=[hbm] * 8,
        out_specs=(hbm,) * 4,
        scratch_shapes=[
            pltpu.VMEM((N_COLS, ROWS), BF),
            pltpu.VMEM((WIDE, HID), BF),
            pltpu.VMEM((WIDE, HID), BF),
            pltpu.VMEM((HID, WIDE), BF),
            pltpu.VMEM((WIDE, HID), BF),
            pltpu.VMEM((WIDE, HID), BF),
            pltpu.VMEM((HID, WIDE), BF),
            pltpu.VMEM((40, HID), F32),
            pltpu.VMEM((40, HID), F32),
            pltpu.VMEM((40, HID), F32),
            pltpu.VMEM((2, 4, ROWS, WIDE), BF),
            pltpu.VMEM((CUT, WIDE), BF),
            pltpu.VMEM((2, WIDE, 2 * HID), BF),
            pltpu.VMEM((2, HID, WIDE), BF),
            pltpu.VMEM((4, 4, CUT, 3 * HID), F32),
            pltpu.VMEM((4, 4, CUT, 3 * HID), BF),
            pltpu.VMEM((4, 4, CUT, 3 * HID), BF),
            pltpu.VMEM((4, CUT, 3 * HID), BF),
            pltpu.VMEM((4, CUT, 3 * HID), BF),
            pltpu.VMEM((4, 2, CUT, 3 * HID), BF),
            pltpu.VMEM((4, 2, CUT, 3 * HID), BF),
            pltpu.VMEM((2, 4, ROWS, 3 * HID), BF),
            pltpu.VMEM((WIDE, 2 * HID), BF),
            pltpu.VMEM((HID, WIDE), BF),
            pltpu.VMEM((WIDE, 2 * HID), BF),
            pltpu.VMEM((HID, WIDE), BF),
            pltpu.VMEM((WIDE, 2 * HID), F32),
            pltpu.VMEM((HID, WIDE), F32),
            pltpu.VMEM((4, 96, WIDE), BF),
            pltpu.VMEM((4, 96, WIDE), BF),
            pltpu.VMEM((4, 96, WIDE), BF),
            pltpu.VMEM((4, 96, WIDE), BF),
            pltpu.VMEM((4, 2, 96, 128), BF),
            pltpu.VMEM((3, 2, 96, 128), BF),
            pltpu.VMEM((2, 96, 128), BF),
            pltpu.VMEM((2, 96, 128), BF),
            pltpu.SemaphoreType.DMA((6,)),
            pltpu.SemaphoreType.DMA((4,)),
            pltpu.SemaphoreType.DMA((136,)),
            pltpu.SemaphoreType.DMA((136,)),
        ],
        compiler_params=pltpu.CompilerParams(
            collective_id=0, has_side_effects=True, vmem_limit_bytes=VMEM_BYTES
        ),
        cost_estimate=pl.CostEstimate(flops=2_100_000_000, bytes_accessed=5_000_000, transcendentals=25_000),
    )(tok, cot, gate_codes, up_codes, down_codes, gate_scales, up_scales, down_scales.T)
    results = pl.pallas_call(
        write_out,
        out_shape=outs,
        in_specs=[hbm] * 4,
        out_specs=(hbm,) * 4,
        scratch_shapes=[pltpu.SemaphoreType.DMA((4,))],
        compiler_params=pltpu.CompilerParams(vmem_limit_bytes=VMEM_BYTES),
    )(*results)
    return (results[0].T,) + tuple(results[1:])


def solution(mesh):
    return jax.shard_map(
        body,
        mesh=mesh,
        in_specs=(
            P("node", None),
            P("node", None),
            P("node", "dp"),
            P("node", "dp"),
            P("dp", "node"),
            P(None, "dp"),
            P(None, "dp"),
            P("dp", None),
        ),
        out_specs=(P("node", "dp"), P("node", "dp"), P("node", "dp"), P("dp", "node")),
        check_vma=False,
    )
```

```python
import jax
import jax.numpy as jnp
from jax import lax
from jax.experimental import pallas as pl
from jax.experimental.pallas import tpu as pltpu
from jax.sharding import PartitionSpec as P

BF = jnp.bfloat16
F32 = jnp.float32
MESH = pl.DeviceIdType.MESH

ROWS = 192
WIDE = 640
HID = 128
QB = 128
CUT = 48
VMEM_BYTES = 60 * 1024 * 1024
SEMS = 144
N_COLS = 80


def dot_nn(a, b):
    return lax.dot_general(a, b, (((1,), (0,)), ((), ())), preferred_element_type=F32)


def dot_nt(a, b):
    return lax.dot_general(a, b, (((1,), (1,)), ((), ())), preferred_element_type=F32)


def dot_tn(a, b):
    return lax.dot_general(a, b, (((0,), (0,)), ((), ())), preferred_element_type=F32)


def kernel(
    tok, cot, gate_codes_hbm, up_codes_hbm, down_codes_hbm, gate_scales_hbm, up_scales_hbm, down_scales_hbm,
    token_grad_hbm, gate_grad_hbm, up_grad_hbm, down_grad_hbm,
    token_grad, gate_grad, up_grad, down_grad, gate_codes, up_codes, down_codes, gate_scales, up_scales, down_scales,
    acts_in, fetch_buf, w_gu, w_down, mine, other, mate_in, sum_out, sum_in,
    hidden, grad_out, down_out, grad_in, down_in, grad_own, down_own,
    ring_buf, ring_in, side_buf, side_in, last_buf, last_in,
    load_sems, store_sems, send_sems, recv_sems,
):
    dp = lax.axis_index("dp")
    node = lax.axis_index("node")
    z, x, low = dp // 8, (dp // 2) % 4, dp % 2
    chip, core = node // 2, node % 2
    par = x % 2
    mate = node + 1 - 2 * core
    pair = dp + 2 - 4 * par
    side = (x // 2) * 2 + low

    def at_z(step):
        return lax.rem(z + step + 8, 8) * 8 + x * 2 + low

    def at_chip(step):
        return lax.rem(chip + step + 4, 4)

    def at_side(member):
        return z * 8 + (par + 2 * (member // 2)) * 2 + member % 2

    loads = [
        pltpu.make_async_copy(src, dst, load_sems.at[i])
        for i, (src, dst) in enumerate((
            (gate_codes_hbm, gate_codes), (up_codes_hbm, up_codes), (down_codes_hbm, down_codes),
            (gate_scales_hbm, gate_scales), (up_scales_hbm, up_scales), (down_scales_hbm, down_scales),
        ))
    ]
    for load in loads:
        load.start()

    counts = {"send": 0, "recv": 0}

    def fresh(kind, number=1):
        first = counts[kind]
        counts[kind] += number
        return first

    sent = []

    def push(src, dst, recv, to_dp, to_node, when=None):
        copy = pltpu.make_async_remote_copy(
            src_ref=src, dst_ref=dst, send_sem=send_sems.at[fresh("send")], recv_sem=recv_sems.at[recv],
            device_id={"dp": to_dp, "node": to_node}, device_id_type=MESH,
        )
        if when is None:
            copy.start()
        else:
            pl.when(when)(copy.start)
        sent.append((copy, when))

    def landed(dst, recv):
        pltpu.make_async_copy(dst, dst, recv_sems.at[recv]).wait()

    barrier = pltpu.get_barrier_semaphore()

    def greet(to_dp, to_node):
        pl.semaphore_signal(barrier, inc=1, device_id={"dp": to_dp, "node": to_node}, device_id_type=MESH)

    for step in range(1, 8):
        greet(dp, lax.rem(node + step, 8))
    greet(at_z(1), node)
    greet(at_z(-1), node)
    greet(pair, node)
    for step in range(1, 4):
        greet(at_side(lax.rem(side + step, 4)), node)
    def last_to(block, cut):
        even = (z + node + 1) % 2
        to_chip = lax.rem(chip + even + 2 * cut, 4)
        return node * 8 + lax.rem(x + block, 4) * 2 + low, to_chip * 2 + par

    def last_from(turn):
        src_chip = z // 2
        even = lax.rem(chip - src_chip + 4, 2)
        src_z = 2 * turn + lax.rem(even + 1 + z, 2)
        src_x = lax.rem(x + 4 - lax.rem(x + core, 2), 4)
        return src_z * 8 + src_x * 2 + low, z

    def is_me(where):
        return jnp.logical_and(where[0] == dp, where[1] == node)

    expected = 13
    for turn in range(4):
        where = last_from(turn)
        pl.when(jnp.logical_not(is_me(where)))(lambda where=where: greet(*where))
    for b in range(2):
        for cut in range(2):
            expected = expected + jnp.where(is_me(last_to(b, cut)), 0, 1)

    for load in loads:
        load.wait()
    eye = lax.broadcasted_iota(jnp.int32, (HID, HID), 0) == lax.broadcasted_iota(jnp.int32, (HID, HID), 1)
    for b in range(WIDE // QB):
        rows = slice(b * QB, (b + 1) * QB)
        line = pl.ds(node * (WIDE // QB) + b, 1)
        w_gu[0, rows, 0:HID] = (gate_codes[rows, :].astype(F32) * gate_scales[line, :]).astype(BF)
        w_gu[0, rows, HID:] = (up_codes[rows, :].astype(F32) * up_scales[line, :]).astype(BF)
        column = jnp.sum(jnp.where(eye, down_scales[line, :], 0.0), axis=1, keepdims=True)
        w_down[0, :, rows] = (down_codes[:, rows].astype(F32) * column).astype(BF)

    pl.semaphore_wait(barrier, expected)

    def quarter_rows(quarter):
        return pl.ds(pl.multiple_of(quarter * CUT, 16), CUT)

    def cols_of(to_node):
        return pl.ds(pl.multiple_of(to_node * WIDE, 128), WIDE)

    is_src = core == par
    fetch_recv = [fresh("recv") for _ in range(3)]
    stage_recv = [fresh("recv") for _ in range(3)]
    own_recv = [fresh("recv") for _ in range(2)]
    own_rows = quarter_rows(z // 2)
    far_steps = (2, 1, 3)
    for a, arr in enumerate((tok, cot)):
        here = jnp.logical_and(is_src, z % 2 == a)
        for step in far_steps:
            push(
                arr.at[own_rows, cols_of(at_chip(step) * 2 + 1 - core)], fetch_buf.at[step - 1],
                stage_recv[step - 1], dp, mate, when=here,
            )
        for step in far_steps:
            to_node = at_chip(step) * 2 + core
            push(
                arr.at[own_rows, cols_of(to_node)], acts_in.at[a, chip, own_rows, :],
                fetch_recv[step - 1], dp, to_node, when=here,
            )

    w_recv = [fresh("recv") for _ in range(2)]
    push(w_gu.at[0], w_gu.at[1], w_recv[0], pair, node)
    push(w_down.at[0], w_down.at[1], w_recv[1], pair, node)

    for a, arr in enumerate((tok, cot)):
        push(arr.at[:, cols_of(mate)], acts_in.at[a, chip], own_recv[a], dp, mate, when=is_src)

        @pl.when(is_src)
        def _(a=a, arr=arr):
            pltpu.make_async_copy(
                arr.at[:, cols_of(node)], acts_in.at[a, chip], recv_sems.at[own_recv[a]]
            ).start()

    not_src = jnp.logical_not(is_src)
    for step in far_steps:
        pl.when(not_src)(lambda step=step: landed(fetch_buf.at[step - 1], stage_recv[step - 1]))
        push(
            fetch_buf.at[step - 1], acts_in.at[z % 2, chip, own_rows, :], fetch_recv[step - 1],
            dp, at_chip(step) * 2 + core, when=not_src,
        )

    up_recv = [[fresh("recv") for _ in range(3)] for _ in range(3)]
    dn_recv = [[fresh("recv") for _ in range(3)] for _ in range(3)]
    far_recv = [fresh("recv") for _ in range(3)]

    def block(turn, step):
        piece = lax.rem(z + turn + 8, 8)
        return acts_in.at[piece % 2, at_chip(-step), quarter_rows(piece // 2), :]

    def relay(turn, step):
        if turn == 0:
            landed(block(0, step), fetch_recv[step - 1])
            push(block(0, step), block(0, step), up_recv[0][step - 1], at_z(1), node)
            push(block(0, step), block(0, step), dn_recv[0][step - 1], at_z(-1), node)
            return
        if turn == 4:
            landed(block(4, step), far_recv[step - 1])
            return
        here = block(-turn, step)
        landed(here, up_recv[turn - 1][step - 1])
        if turn < 3:
            push(here, here, up_recv[turn][step - 1], at_z(1), node)
        elif step != 3:
            push(here, here, far_recv[step - 1], at_z(1), node, when=None if step == 1 else core == 0)
        here = block(turn, step)
        landed(here, dn_recv[turn - 1][step - 1])
        if turn < 3:
            push(here, here, dn_recv[turn][step - 1], at_z(-1), node)
        elif step != 1:
            push(here, here, far_recv[step - 1], at_z(-1), node, when=None if step == 3 else core == 1)

    sign = 1 - 2 * (z % 2)
    quarters = [
        lax.rem(z + first * sign + 8, 8) // 2 for first in (0, -1, 2, -3)
    ]
    mate_recv = [fresh("recv") for _ in range(4)]
    sum_recv = [[fresh("recv") for _ in range(3)] for _ in range(4)]
    hid_recv = [[fresh("recv") for _ in range(3)] for _ in range(4)]
    hid_mate = [[fresh("recv") for _ in range(4)] for _ in range(4)]

    def multiply(s):
        rows = quarter_rows(quarters[s])
        tokens = acts_in[0, :, rows, :].reshape(4 * CUT, WIDE)
        grads = acts_in[1, :, rows, :].reshape(4 * CUT, WIDE)
        for part, store in ((1 - core, other), (core, mine)):
            store[s, :, :, 0 : 2 * HID] = (
                dot_nn(tokens, w_gu[part]).reshape(4, CUT, 2 * HID).astype(store.dtype)
            )
            store[s, :, :, 2 * HID :] = (
                dot_nt(grads, w_down[part]).reshape(4, CUT, HID).astype(store.dtype)
            )
            if store is other:
                push(other.at[s], mate_in.at[s], mate_recv[s], dp, mate)

    def combine(s):
        landed(mate_in.at[s], mate_recv[s])
        for step in far_steps:
            to = at_chip(step)
            sum_out[s, step - 1] = (mine[s, to] + mate_in[s, to].astype(F32)).astype(BF)
            push(
                sum_out.at[s, step - 1], sum_in.at[s, step - 1], sum_recv[s][step - 1],
                dp, to * 2 + core,
            )

    def activate(s):
        full = mine[s, chip] + mate_in[s, chip].astype(F32)
        for i in (0, 2, 1):
            landed(sum_in.at[s, i], sum_recv[s][i])
            full = full + sum_in[s, i].astype(F32)
        rows = quarter_rows(quarters[s])
        gate, upper, d_act = full[:, 0:HID], full[:, HID : 2 * HID], full[:, 2 * HID :]
        sig = jax.nn.sigmoid(gate)
        silu = gate * sig
        hidden[core, chip, rows, 0:HID] = (d_act * upper * sig * (1.0 + gate * (1.0 - sig))).astype(BF)
        hidden[core, chip, rows, HID : 2 * HID] = (d_act * silu).astype(BF)
        hidden[core, chip, rows, 2 * HID :] = (silu * upper).astype(BF)
        own = hidden.at[core, chip, rows]
        for step in far_steps:
            push(own, own, hid_recv[s][step - 1], dp, at_chip(step) * 2 + core)
        push(own, own, hid_mate[s][0], dp, mate)

    def forward_hidden(s):
        rows = quarter_rows(quarters[s])
        for step in (1, 3, 2):
            here = hidden.at[core, at_chip(-step), rows]
            landed(here, hid_recv[s][step - 1])
            push(here, here, hid_mate[s][step], dp, mate)

    def finish_hidden(s):
        rows = quarter_rows(quarters[s])
        for step in range(4):
            landed(hidden.at[1 - core, at_chip(-step), rows], hid_mate[s][step])

    ring_slot = {-3: 0, 3: 1, -2: 2, 2: 3, -1: 4, 1: 5, 0: 6}
    ring_recv = [[fresh("recv") for _ in range(2)] for _ in range(8)]
    buf_slot = {4: 0, 3: 1, -3: 2, 2: 3, -2: 4, 1: 5, -1: 6}
    pairs = ((4, -3), (2, 3), (-2, -1), (0, 1))

    def cut_rows(cut):
        return slice(cut * CUT, (cut + 1) * CUT)

    def token_terms(s, i):
        half = lax.rem(i + z, 2)
        even = lax.rem(half + node + 1, 2)
        rows = quarter_rows(quarters[s])
        total = None
        for part in range(2):
            data = jnp.concatenate(
                [hidden[part, lax.rem(chip + even + 2 * cut, 4), rows, 0 : 2 * HID] for cut in range(2)], axis=0
            )
            term = dot_nt(data, w_gu[part])
            total = term if total is None else total + term
        return total

    def chain(far):
        s, i = [(s, pair.index(far)) for s, pair in enumerate(pairs) if far in pair][0]
        terms = token_terms(s, i)
        if far == 0:
            return terms
        way = 1 if far > 0 else -1
        buf = buf_slot[far]
        for cut in range(2):
            rows = cut_rows(cut)
            value = terms[rows]
            if abs(far) < 3 or far == (-3, 3)[cut]:
                slot = ring_slot[far]
                landed(ring_in.at[slot, rows], ring_recv[slot][cut])
                value = value + ring_in[slot, rows].astype(F32)
            ring_buf[buf, rows] = value.astype(BF)
            if far == 4:
                to, slot = sign * (1 - 2 * cut), (0, 1)[cut]
            else:
                to, slot = sign * way, 7 if far == -1 else ring_slot[-(far - way)]
            push(ring_buf.at[buf, rows], ring_in.at[slot, rows], ring_recv[slot][cut], at_z(to), node)
        return None

    for step in (1, 3, 2):
        relay(0, step)
    relay(1, 1)
    relay(1, 3)
    for a in range(2):
        landed(acts_in.at[a, chip], own_recv[a])
    relay(1, 2)
    landed(w_gu.at[1], w_recv[0])
    landed(w_down.at[1], w_recv[1])
    multiply(0)
    relay(2, 1)
    combine(0)
    relay(2, 3)
    relay(2, 2)
    multiply(1)
    relay(3, 1)
    combine(1)
    relay(3, 3)
    relay(3, 2)
    multiply(2)
    activate(0)
    relay(4, 1)
    combine(2)
    relay(4, 3)
    relay(4, 2)
    multiply(3)
    activate(1)
    combine(3)
    forward_hidden(0)
    activate(2)
    finish_hidden(0)
    chain(4)
    forward_hidden(1)
    activate(3)
    finish_hidden(1)
    chain(-3)
    chain(3)
    chain(2)
    forward_hidden(2)
    finish_hidden(2)
    chain(-2)
    chain(-1)
    forward_hidden(3)
    finish_hidden(3)
    chain(1)

    def weight_grads(part):
        tokens = acts_in[0].reshape(4 * ROWS, WIDE)
        grads = acts_in[1].reshape(4 * ROWS, WIDE)
        back = hidden[part].reshape(4 * ROWS, 3 * HID)
        return dot_tn(tokens, back[:, 0 : 2 * HID]), dot_tn(back[:, 2 * HID :], grads)

    first, second = weight_grads(1)
    grad_out[...] = first.astype(BF)
    down_out[...] = second.astype(BF)
    grad_recv = [fresh("recv") for _ in range(2)]
    push(grad_out, grad_in, grad_recv[0], pair, node)
    push(down_out, down_in, grad_recv[1], pair, node)

    terms = chain(0)

    first, second = weight_grads(0)
    grad_own[...] = first
    down_own[...] = second

    for slot in (7, 6):
        for cut in range(2):
            landed(ring_in.at[slot, cut_rows(cut)], ring_recv[slot][cut])
    terms = terms + ring_in[6].astype(F32) + ring_in[7].astype(F32)
    for i in range(8):
        turn = lax.rem(i // 2 - par + 4, 4)
        member, b = (turn // 2) * 2 + i % 2, lax.rem(turn, 2)
        side_buf[member, b, :, 0:N_COLS] = terms[:, i * N_COLS : (i + 1) * N_COLS].astype(BF)
        side_buf[member, b, :, N_COLS:] = jnp.zeros((96, 128 - N_COLS), BF)

    side_recv = [fresh("recv") for _ in range(3)]
    for step in range(1, 4):
        to = lax.rem(side + step, 4)
        push(side_buf.at[to], side_in.at[step - 1], side_recv[step - 1], at_side(to), node)
    total = side_buf[side].astype(F32)
    for step in range(1, 4):
        landed(side_in.at[step - 1], side_recv[step - 1])
        total = total + side_in[step - 1].astype(F32)
    last_buf[...] = total.astype(BF)

    last_recv = fresh("recv", 4)
    quarter = lax.rem(z // 2 + 2, 4)
    for b in range(2):
        for cut in range(2):
            where = last_to(b, cut)
            src, dst, recv = last_buf.at[b, cut_rows(cut)], last_in.at[quarter], last_recv + quarter
            push(src, dst, recv, *where, when=jnp.logical_not(is_me(where)))

            @pl.when(is_me(where))
            def _(src=src, dst=dst, recv=recv):
                pltpu.make_async_copy(src, dst, recv_sems.at[recv]).start()

    landed(grad_in, grad_recv[0])
    landed(down_in, grad_recv[1])
    gate_grad[...] = (grad_own[:, 0:HID] + grad_in[:, 0:HID].astype(F32)).astype(BF)
    up_grad[...] = (grad_own[:, HID:] + grad_in[:, HID:].astype(F32)).astype(BF)
    down_grad[...] = (down_own[...] + down_in[...].astype(F32)).astype(BF)
    stores = [
        pltpu.make_async_copy(src, dst, store_sems.at[i])
        for i, (src, dst) in enumerate((
            (gate_grad, gate_grad_hbm), (up_grad, up_grad_hbm), (down_grad, down_grad_hbm),
            (token_grad, token_grad_hbm),
        ))
    ]
    for store in stores[:3]:
        store.start()

    for i in range(4):
        landed(last_in.at[i], last_recv + i)
    token_grad[...] = jnp.transpose(last_in[...].reshape(ROWS, 128).astype(F32))[0:N_COLS, :].astype(BF)
    stores[3].start()

    assert max(counts.values()) <= SEMS

    for copy, when in sent:
        if when is None:
            copy.wait_send()
        else:
            pl.when(when)(copy.wait_send)
    for store in stores:
        store.wait()


def write_out(*refs):
    for src, dst in zip(refs[:4], refs[4:]):
        dst[...] = src[...]


def body(tok, cot, gate_codes, up_codes, down_codes, gate_scales, up_scales, down_scales):
    hbm = pl.BlockSpec(memory_space=pltpu.HBM)
    outs = (
        jax.ShapeDtypeStruct((N_COLS, ROWS), BF),
        jax.ShapeDtypeStruct((WIDE, HID), BF),
        jax.ShapeDtypeStruct((WIDE, HID), BF),
        jax.ShapeDtypeStruct((HID, WIDE), BF),
    )
    results = pl.pallas_call(
        kernel,
        out_shape=outs,
        in_specs=[hbm] * 8,
        out_specs=(hbm,) * 4,
        scratch_shapes=[
            pltpu.VMEM((N_COLS, ROWS), BF),
            pltpu.VMEM((WIDE, HID), BF),
            pltpu.VMEM((WIDE, HID), BF),
            pltpu.VMEM((HID, WIDE), BF),
            pltpu.VMEM((WIDE, HID), BF),
            pltpu.VMEM((WIDE, HID), BF),
            pltpu.VMEM((HID, WIDE), BF),
            pltpu.VMEM((40, HID), F32),
            pltpu.VMEM((40, HID), F32),
            pltpu.VMEM((40, HID), F32),
            pltpu.VMEM((2, 4, ROWS, WIDE), BF),
            pltpu.VMEM((3, CUT, WIDE), BF),
            pltpu.VMEM((2, WIDE, 2 * HID), BF),
            pltpu.VMEM((2, HID, WIDE), BF),
            pltpu.VMEM((4, 4, CUT, 3 * HID), F32),
            pltpu.VMEM((4, 4, CUT, 3 * HID), BF),
            pltpu.VMEM((4, 4, CUT, 3 * HID), BF),
            pltpu.VMEM((4, 3, CUT, 3 * HID), BF),
            pltpu.VMEM((4, 3, CUT, 3 * HID), BF),
            pltpu.VMEM((2, 4, ROWS, 3 * HID), BF),
            pltpu.VMEM((WIDE, 2 * HID), BF),
            pltpu.VMEM((HID, WIDE), BF),
            pltpu.VMEM((WIDE, 2 * HID), BF),
            pltpu.VMEM((HID, WIDE), BF),
            pltpu.VMEM((WIDE, 2 * HID), F32),
            pltpu.VMEM((HID, WIDE), F32),
            pltpu.VMEM((7, 96, WIDE), BF),
            pltpu.VMEM((8, 96, WIDE), BF),
            pltpu.VMEM((4, 2, 96, 128), BF),
            pltpu.VMEM((3, 2, 96, 128), BF),
            pltpu.VMEM((2, 96, 128), BF),
            pltpu.VMEM((4, CUT, 128), BF),
            pltpu.SemaphoreType.DMA((6,)),
            pltpu.SemaphoreType.DMA((4,)),
            pltpu.SemaphoreType.DMA((SEMS,)),
            pltpu.SemaphoreType.DMA((SEMS,)),
        ],
        compiler_params=pltpu.CompilerParams(
            collective_id=0, has_side_effects=True, vmem_limit_bytes=VMEM_BYTES
        ),
        cost_estimate=pl.CostEstimate(flops=2_100_000_000, bytes_accessed=5_000_000, transcendentals=25_000),
    )(tok, cot, gate_codes, up_codes, down_codes, gate_scales, up_scales, down_scales.T)
    results = pl.pallas_call(
        write_out,
        out_shape=outs,
        compiler_params=pltpu.CompilerParams(vmem_limit_bytes=VMEM_BYTES),
    )(*results)
    return (results[0].T,) + tuple(results[1:])


def solution(mesh):
    return jax.shard_map(
        body,
        mesh=mesh,
        in_specs=(
            P("node", None),
            P("node", None),
            P("node", "dp"),
            P("node", "dp"),
            P("dp", "node"),
            P(None, "dp"),
            P(None, "dp"),
            P("dp", None),
        ),
        out_specs=(P("node", "dp"), P("node", "dp"), P("node", "dp"), P("dp", "node")),
        check_vma=False,
    )
```

```python
import jax
import jax.numpy as jnp
from jax import lax
from jax.experimental import pallas as pl
from jax.experimental.pallas import tpu as pltpu
from jax.sharding import PartitionSpec as P

BF = jnp.bfloat16
F32 = jnp.float32
MESH = pl.DeviceIdType.MESH

ROWS = 192
WIDE = 640
HID = 128
QB = 128
CUT = 48
VMEM_BYTES = 60 * 1024 * 1024
SEMS = 144
N_COLS = 80


def dot_nn(a, b):
    return lax.dot_general(a, b, (((1,), (0,)), ((), ())), preferred_element_type=F32)


def dot_nt(a, b):
    return lax.dot_general(a, b, (((1,), (1,)), ((), ())), preferred_element_type=F32)


def dot_tn(a, b):
    return lax.dot_general(a, b, (((0,), (0,)), ((), ())), preferred_element_type=F32)


def kernel(
    tok, cot, gate_codes_hbm, up_codes_hbm, down_codes_hbm, gate_scales_hbm, up_scales_hbm, down_scales_hbm,
    token_grad_hbm, gate_grad_hbm, up_grad_hbm, down_grad_hbm,
    token_grad, gate_grad, up_grad, down_grad, gate_codes, up_codes, down_codes, gate_scales, up_scales, down_scales,
    acts_in, fetch_buf, w_gu, w_down, mine, other, mate_in, sum_out, sum_in,
    hidden, grad_out, down_out, grad_in, down_in, grad_own, down_own,
    ring_buf, ring_in, side_buf, side_in, last_buf, last_in,
    load_sems, store_sems, send_sems, recv_sems,
):
    dp = lax.axis_index("dp")
    node = lax.axis_index("node")
    z, x, low = dp // 8, (dp // 2) % 4, dp % 2
    chip, core = node // 2, node % 2
    par = x % 2
    mate = node + 1 - 2 * core
    pair = dp + 2 - 4 * par
    side = (x // 2) * 2 + low

    def at_z(step):
        return lax.rem(z + step + 8, 8) * 8 + x * 2 + low

    def at_chip(step):
        return lax.rem(chip + step + 4, 4)

    def at_side(member):
        return z * 8 + (par + 2 * (member // 2)) * 2 + member % 2

    loads = [
        pltpu.make_async_copy(src, dst, load_sems.at[i])
        for i, (src, dst) in enumerate((
            (gate_codes_hbm, gate_codes), (up_codes_hbm, up_codes), (down_codes_hbm, down_codes),
            (gate_scales_hbm, gate_scales), (up_scales_hbm, up_scales), (down_scales_hbm, down_scales),
        ))
    ]
    for load in loads:
        load.start()

    counts = {"send": 0, "recv": 0}

    def fresh(kind, number=1):
        first = counts[kind]
        counts[kind] += number
        return first

    sent = []

    def push(src, dst, recv, to_dp, to_node, when=None):
        copy = pltpu.make_async_remote_copy(
            src_ref=src, dst_ref=dst, send_sem=send_sems.at[fresh("send")], recv_sem=recv_sems.at[recv],
            device_id={"dp": to_dp, "node": to_node}, device_id_type=MESH,
        )
        if when is None:
            copy.start()
        else:
            pl.when(when)(copy.start)
        sent.append((copy, when))

    def landed(dst, recv):
        pltpu.make_async_copy(dst, dst, recv_sems.at[recv]).wait()

    barrier = pltpu.get_barrier_semaphore()

    def greet(to_dp, to_node):
        pl.semaphore_signal(barrier, inc=1, device_id={"dp": to_dp, "node": to_node}, device_id_type=MESH)

    for step in range(1, 8):
        greet(dp, lax.rem(node + step, 8))
    greet(at_z(1), node)
    greet(at_z(-1), node)
    greet(at_z(4), node)
    greet(pair, node)
    for step in range(1, 4):
        greet(at_side(lax.rem(side + step, 4)), node)
    def half_at(where, origin):
        return lax.rem(where - origin + 18, 8) // 4

    def last_to(block, cut):
        to_chip = lax.rem(chip + half_at(z, node) + 2 * cut, 4)
        return node * 8 + lax.rem(x + block, 4) * 2 + low, to_chip * 2 + par

    def last_from(quarter):
        half = lax.rem(chip - z // 2 + 4, 2)
        swap = lax.rem(half_at(quarter + 2, z) + half, 2)
        src_x = lax.rem(x + 4 - lax.rem(x + core, 2), 4)
        return lax.rem(quarter + 2 + 4 * swap, 8) * 8 + src_x * 2 + low, z

    def is_me(where):
        return jnp.logical_and(where[0] == dp, where[1] == node)

    expected = 14
    for turn in range(4):
        where = last_from(turn)
        pl.when(jnp.logical_not(is_me(where)))(lambda where=where: greet(*where))
    for b in range(2):
        for cut in range(2):
            expected = expected + jnp.where(is_me(last_to(b, cut)), 0, 1)

    for load in loads:
        load.wait()
    eye = lax.broadcasted_iota(jnp.int32, (HID, HID), 0) == lax.broadcasted_iota(jnp.int32, (HID, HID), 1)
    for b in range(WIDE // QB):
        rows = slice(b * QB, (b + 1) * QB)
        line = pl.ds(node * (WIDE // QB) + b, 1)
        w_gu[0, rows, 0:HID] = (gate_codes[rows, :].astype(F32) * gate_scales[line, :]).astype(BF)
        w_gu[0, rows, HID:] = (up_codes[rows, :].astype(F32) * up_scales[line, :]).astype(BF)
        column = jnp.sum(jnp.where(eye, down_scales[line, :], 0.0), axis=1, keepdims=True)
        w_down[0, :, rows] = (down_codes[:, rows].astype(F32) * column).astype(BF)

    pl.semaphore_wait(barrier, expected)

    def quarter_rows(quarter):
        return pl.ds(pl.multiple_of(quarter * CUT, 16), CUT)

    def cols_of(to_node):
        return pl.ds(pl.multiple_of(to_node * WIDE, 128), WIDE)

    is_src = core == par
    fetch_recv = [[fresh("recv") for _ in range(3)] for _ in range(2)]
    stage_recv = [[fresh("recv") for _ in range(3)] for _ in range(2)]
    own_recv = [fresh("recv") for _ in range(2)]
    own_rows = quarter_rows(z % 4)
    far_steps = (2, 1, 3)
    items = ((0, 1), (1, 3), (1, 1), (0, 3), (0, 2), (1, 2))
    for a, step in items:
        push(
            (tok, cot)[a].at[own_rows, cols_of(at_chip(step) * 2 + 1 - core)], fetch_buf.at[a, step - 1],
            stage_recv[a][step - 1], dp, mate, when=is_src,
        )
    for a, step in items:
        to_node = at_chip(step) * 2 + core
        push(
            (tok, cot)[a].at[own_rows, cols_of(to_node)], acts_in.at[a, chip, own_rows, :],
            fetch_recv[a][step - 1], dp, to_node, when=is_src,
        )

    w_recv = [fresh("recv") for _ in range(2)]
    push(w_gu.at[0], w_gu.at[1], w_recv[0], pair, node)
    push(w_down.at[0], w_down.at[1], w_recv[1], pair, node)

    for a, arr in enumerate((tok, cot)):
        push(arr.at[:, cols_of(mate)], acts_in.at[a, chip], own_recv[a], dp, mate, when=is_src)

        @pl.when(is_src)
        def _(a=a, arr=arr):
            pltpu.make_async_copy(
                arr.at[:, cols_of(node)], acts_in.at[a, chip], recv_sems.at[own_recv[a]]
            ).start()

    not_src = jnp.logical_not(is_src)
    for a, step in items:
        pl.when(not_src)(lambda a=a, step=step: landed(fetch_buf.at[a, step - 1], stage_recv[a][step - 1]))
        push(
            fetch_buf.at[a, step - 1], acts_in.at[a, chip, own_rows, :], fetch_recv[a][step - 1],
            dp, at_chip(step) * 2 + core, when=not_src,
        )

    up_recv = [[fresh("recv") for _ in range(3)] for _ in range(2)]
    dn_recv = [[fresh("recv") for _ in range(3)] for _ in range(2)]
    far_recv = [[fresh("recv") for _ in range(3)] for _ in range(2)]

    def block(turn, item):
        a, step = items[item]
        return acts_in.at[a, at_chip(-step), quarter_rows(lax.rem(z + turn + 4, 4)), :]

    def relay(turn, item):
        a, step = items[item]
        if turn == 0:
            here = block(0, item)
            landed(here, fetch_recv[a][step - 1])
            push(here, here, up_recv[a][step - 1], at_z(1), node)
            push(here, here, dn_recv[a][step - 1], at_z(-1), node)
        elif turn == 1:
            here = block(-1, item)
            landed(here, up_recv[a][step - 1])
            if a == 0:
                push(here, here, far_recv[a][step - 1], at_z(1), node)
            here = block(1, item)
            landed(here, dn_recv[a][step - 1])
            if a == 1:
                push(here, here, far_recv[a][step - 1], at_z(-1), node)
        else:
            landed(block(2, item), far_recv[a][step - 1])

    quarters = [lax.rem(z + turn, 4) for turn in (0, 1, 3, 2)]
    mate_recv = [fresh("recv") for _ in range(4)]
    sum_recv = [[fresh("recv") for _ in range(3)] for _ in range(4)]
    hid_recv = [[fresh("recv") for _ in range(3)] for _ in range(4)]
    hid_mate = [[fresh("recv") for _ in range(4)] for _ in range(4)]

    def multiply(s):
        rows = quarter_rows(quarters[s])
        tokens = acts_in[0, :, rows, :].reshape(4 * CUT, WIDE)
        grads = acts_in[1, :, rows, :].reshape(4 * CUT, WIDE)
        for part, store in ((1 - core, other), (core, mine)):
            store[s, :, :, 0 : 2 * HID] = (
                dot_nn(tokens, w_gu[part]).reshape(4, CUT, 2 * HID).astype(store.dtype)
            )
            store[s, :, :, 2 * HID :] = (
                dot_nt(grads, w_down[part]).reshape(4, CUT, HID).astype(store.dtype)
            )
            if store is other:
                push(other.at[s], mate_in.at[s], mate_recv[s], dp, mate)

    def combine(s):
        landed(mate_in.at[s], mate_recv[s])
        for step in far_steps:
            to = at_chip(step)
            sum_out[s, step - 1] = (mine[s, to] + mate_in[s, to].astype(F32)).astype(BF)
            push(
                sum_out.at[s, step - 1], sum_in.at[s, step - 1], sum_recv[s][step - 1],
                dp, to * 2 + core,
            )

    def activate(s):
        full = mine[s, chip] + mate_in[s, chip].astype(F32)
        for i in (0, 2, 1):
            landed(sum_in.at[s, i], sum_recv[s][i])
            full = full + sum_in[s, i].astype(F32)
        rows = quarter_rows(quarters[s])
        gate, upper, d_act = full[:, 0:HID], full[:, HID : 2 * HID], full[:, 2 * HID :]
        sig = jax.nn.sigmoid(gate)
        silu = gate * sig
        hidden[core, chip, rows, 0:HID] = (d_act * upper * sig * (1.0 + gate * (1.0 - sig))).astype(BF)
        hidden[core, chip, rows, HID : 2 * HID] = (d_act * silu).astype(BF)
        hidden[core, chip, rows, 2 * HID :] = (silu * upper).astype(BF)
        own = hidden.at[core, chip, rows]
        for step in far_steps:
            push(own, own, hid_recv[s][step - 1], dp, at_chip(step) * 2 + core)
        push(own, own, hid_mate[s][0], dp, mate)

    def forward_hidden(s):
        rows = quarter_rows(quarters[s])
        for step in (1, 3, 2):
            here = hidden.at[core, at_chip(-step), rows]
            landed(here, hid_recv[s][step - 1])
            push(here, here, hid_mate[s][step], dp, mate)

    def finish_hidden(s):
        rows = quarter_rows(quarters[s])
        for step in range(4):
            landed(hidden.at[1 - core, at_chip(-step), rows], hid_mate[s][step])

    ring_slot = {2: 0, 1: 1, -2: 2, -1: 3, (0, 1): 4, (0, -1): 5, (0, 4): 6}
    ring_recv = [[fresh("recv") for _ in range(2)] for _ in range(7)]
    buf_slot = {4: 0, 3: 1, -3: 2, 2: 3, -2: 4, 1: 5, -1: 6}
    pairs = ((2, -2), (3, -1), (1, -3), (4, 0))

    def cut_rows(cut):
        return slice(cut * CUT, (cut + 1) * CUT)

    def token_terms(s, far):
        half = half_at(z + far, node)
        rows = quarter_rows(quarters[s])
        total = None
        for part in range(2):
            data = jnp.concatenate(
                [hidden[part, lax.rem(chip + half + 2 * cut, 4), rows, 0 : 2 * HID] for cut in range(2)], axis=0
            )
            term = dot_nt(data, w_gu[part])
            total = term if total is None else total + term
        return total

    def chain(far):
        s = [s for s, pair in enumerate(pairs) if far in pair][0]
        terms = token_terms(s, far)
        if far == 0:
            return terms
        way = 1 if far > 0 else -1
        to, buf = (4 if far == 4 else way), buf_slot[far]
        into = ring_slot[far - way] if 1 < abs(far) < 4 else ring_slot[0, far]
        for cut in range(2):
            rows = cut_rows(cut)
            value = terms[rows]
            if abs(far) < 3:
                slot = ring_slot[far]
                landed(ring_in.at[slot, rows], ring_recv[slot][cut])
                value = value + ring_in[slot, rows].astype(F32)
            ring_buf[buf, rows] = value.astype(BF)
            push(ring_buf.at[buf, rows], ring_in.at[into, rows], ring_recv[into][cut], at_z(to), node)
        return None

    relay(0, 0)
    relay(0, 1)
    relay(0, 2)
    relay(1, 0)
    relay(0, 3)
    relay(1, 1)
    relay(0, 4)
    relay(1, 2)
    relay(0, 5)
    for a in range(2):
        landed(acts_in.at[a, chip], own_recv[a])
    landed(w_gu.at[1], w_recv[0])
    landed(w_down.at[1], w_recv[1])
    multiply(0)
    relay(1, 3)
    relay(1, 4)
    combine(0)
    relay(1, 5)
    multiply(1)
    multiply(2)
    combine(1)
    combine(2)
    for item in range(6):
        relay(2, item)
    multiply(3)
    activate(0)
    combine(3)
    forward_hidden(0)
    activate(1)
    activate(2)
    finish_hidden(0)
    forward_hidden(1)
    activate(3)
    forward_hidden(2)
    finish_hidden(1)
    chain(3)
    finish_hidden(2)
    chain(-3)
    chain(2)
    forward_hidden(3)
    chain(1)
    chain(-2)
    finish_hidden(3)
    chain(4)
    chain(-1)

    def weight_grads(part):
        tokens = acts_in[0].reshape(4 * ROWS, WIDE)
        grads = acts_in[1].reshape(4 * ROWS, WIDE)
        back = hidden[part].reshape(4 * ROWS, 3 * HID)
        return dot_tn(tokens, back[:, 0 : 2 * HID]), dot_tn(back[:, 2 * HID :], grads)

    first, second = weight_grads(1)
    grad_out[...] = first.astype(BF)
    down_out[...] = second.astype(BF)
    grad_recv = [fresh("recv") for _ in range(2)]
    push(grad_out, grad_in, grad_recv[0], pair, node)
    push(down_out, down_in, grad_recv[1], pair, node)

    terms = chain(0)

    first, second = weight_grads(0)
    grad_own[...] = first
    down_own[...] = second

    for slot in (4, 5, 6):
        for cut in range(2):
            landed(ring_in.at[slot, cut_rows(cut)], ring_recv[slot][cut])
        terms = terms + ring_in[slot].astype(F32)
    for i in range(8):
        turn = lax.rem(i // 2 - par + 4, 4)
        member, b = (turn // 2) * 2 + i % 2, lax.rem(turn, 2)
        side_buf[member, b, :, 0:N_COLS] = terms[:, i * N_COLS : (i + 1) * N_COLS].astype(BF)
        side_buf[member, b, :, N_COLS:] = jnp.zeros((96, 128 - N_COLS), BF)

    side_recv = [fresh("recv") for _ in range(3)]
    for step in range(1, 4):
        to = lax.rem(side + step, 4)
        push(side_buf.at[to], side_in.at[step - 1], side_recv[step - 1], at_side(to), node)
    total = side_buf[side].astype(F32)
    for step in range(1, 4):
        landed(side_in.at[step - 1], side_recv[step - 1])
        total = total + side_in[step - 1].astype(F32)
    last_buf[...] = total.astype(BF)

    last_recv = fresh("recv", 4)
    quarter = lax.rem(z + 2, 4)
    for b in range(2):
        for cut in range(2):
            where = last_to(b, cut)
            src, dst, recv = last_buf.at[b, cut_rows(cut)], last_in.at[quarter], last_recv + quarter
            push(src, dst, recv, *where, when=jnp.logical_not(is_me(where)))

            @pl.when(is_me(where))
            def _(src=src, dst=dst, recv=recv):
                pltpu.make_async_copy(src, dst, recv_sems.at[recv]).start()

    landed(grad_in, grad_recv[0])
    landed(down_in, grad_recv[1])
    gate_grad[...] = (grad_own[:, 0:HID] + grad_in[:, 0:HID].astype(F32)).astype(BF)
    up_grad[...] = (grad_own[:, HID:] + grad_in[:, HID:].astype(F32)).astype(BF)
    down_grad[...] = (down_own[...] + down_in[...].astype(F32)).astype(BF)
    stores = [
        pltpu.make_async_copy(src, dst, store_sems.at[i])
        for i, (src, dst) in enumerate((
            (gate_grad, gate_grad_hbm), (up_grad, up_grad_hbm), (down_grad, down_grad_hbm),
            (token_grad, token_grad_hbm),
        ))
    ]
    for store in stores[:3]:
        store.start()

    for i in range(4):
        landed(last_in.at[i], last_recv + i)
    token_grad[...] = jnp.transpose(last_in[...].reshape(ROWS, 128).astype(F32))[0:N_COLS, :].astype(BF)
    stores[3].start()

    assert max(counts.values()) <= SEMS

    for copy, when in sent:
        if when is None:
            copy.wait_send()
        else:
            pl.when(when)(copy.wait_send)
    for store in stores:
        store.wait()


def write_out(*refs):
    for src, dst in zip(refs[:4], refs[4:]):
        dst[...] = src[...]


def body(tok, cot, gate_codes, up_codes, down_codes, gate_scales, up_scales, down_scales):
    hbm = pl.BlockSpec(memory_space=pltpu.HBM)
    outs = (
        jax.ShapeDtypeStruct((N_COLS, ROWS), BF),
        jax.ShapeDtypeStruct((WIDE, HID), BF),
        jax.ShapeDtypeStruct((WIDE, HID), BF),
        jax.ShapeDtypeStruct((HID, WIDE), BF),
    )
    results = pl.pallas_call(
        kernel,
        out_shape=outs,
        in_specs=[hbm] * 8,
        out_specs=(hbm,) * 4,
        scratch_shapes=[
            pltpu.VMEM((N_COLS, ROWS), BF),
            pltpu.VMEM((WIDE, HID), BF),
            pltpu.VMEM((WIDE, HID), BF),
            pltpu.VMEM((HID, WIDE), BF),
            pltpu.VMEM((WIDE, HID), BF),
            pltpu.VMEM((WIDE, HID), BF),
            pltpu.VMEM((HID, WIDE), BF),
            pltpu.VMEM((40, HID), F32),
            pltpu.VMEM((40, HID), F32),
            pltpu.VMEM((40, HID), F32),
            pltpu.VMEM((2, 4, ROWS, WIDE), BF),
            pltpu.VMEM((2, 3, CUT, WIDE), BF),
            pltpu.VMEM((2, WIDE, 2 * HID), BF),
            pltpu.VMEM((2, HID, WIDE), BF),
            pltpu.VMEM((4, 4, CUT, 3 * HID), F32),
            pltpu.VMEM((4, 4, CUT, 3 * HID), BF),
            pltpu.VMEM((4, 4, CUT, 3 * HID), BF),
            pltpu.VMEM((4, 3, CUT, 3 * HID), BF),
            pltpu.VMEM((4, 3, CUT, 3 * HID), BF),
            pltpu.VMEM((2, 4, ROWS, 3 * HID), BF),
            pltpu.VMEM((WIDE, 2 * HID), BF),
            pltpu.VMEM((HID, WIDE), BF),
            pltpu.VMEM((WIDE, 2 * HID), BF),
            pltpu.VMEM((HID, WIDE), BF),
            pltpu.VMEM((WIDE, 2 * HID), F32),
            pltpu.VMEM((HID, WIDE), F32),
            pltpu.VMEM((7, 96, WIDE), BF),
            pltpu.VMEM((7, 96, WIDE), BF),
            pltpu.VMEM((4, 2, 96, 128), BF),
            pltpu.VMEM((3, 2, 96, 128), BF),
            pltpu.VMEM((2, 96, 128), BF),
            pltpu.VMEM((4, CUT, 128), BF),
            pltpu.SemaphoreType.DMA((6,)),
            pltpu.SemaphoreType.DMA((4,)),
            pltpu.SemaphoreType.DMA((SEMS,)),
            pltpu.SemaphoreType.DMA((SEMS,)),
        ],
        compiler_params=pltpu.CompilerParams(
            collective_id=0, has_side_effects=True, vmem_limit_bytes=VMEM_BYTES
        ),
        cost_estimate=pl.CostEstimate(flops=2_100_000_000, bytes_accessed=5_000_000, transcendentals=25_000),
    )(tok, cot, gate_codes, up_codes, down_codes, gate_scales, up_scales, down_scales.T)
    results = pl.pallas_call(
        write_out,
        out_shape=outs,
        compiler_params=pltpu.CompilerParams(vmem_limit_bytes=VMEM_BYTES),
    )(*results)
    return (results[0].T,) + tuple(results[1:])


def solution(mesh):
    return jax.shard_map(
        body,
        mesh=mesh,
        in_specs=(
            P("node", None),
            P("node", None),
            P("node", "dp"),
            P("node", "dp"),
            P("dp", "node"),
            P(None, "dp"),
            P(None, "dp"),
            P("dp", None),
        ),
        out_specs=(P("node", "dp"), P("node", "dp"), P("node", "dp"), P("dp", "node")),
        check_vma=False,
    )
```

```python
import jax
import jax.numpy as jnp
from jax import lax
from jax.experimental import pallas as pl
from jax.experimental.pallas import tpu as pltpu
from jax.sharding import PartitionSpec as P

BF = jnp.bfloat16
F32 = jnp.float32
MESH = pl.DeviceIdType.MESH

ROWS = 192
WIDE = 640
HID = 128
QB = 128
CUT = 48
VMEM_BYTES = 60 * 1024 * 1024
SEMS = 144
N_COLS = 80


def dot_nn(a, b):
    return lax.dot_general(a, b, (((1,), (0,)), ((), ())), preferred_element_type=F32)


def dot_nt(a, b):
    return lax.dot_general(a, b, (((1,), (1,)), ((), ())), preferred_element_type=F32)


def dot_tn(a, b):
    return lax.dot_general(a, b, (((0,), (0,)), ((), ())), preferred_element_type=F32)


def kernel(
    tok, cot, gate_codes_hbm, up_codes_hbm, down_codes_hbm, gate_scales_hbm, up_scales_hbm, down_scales_hbm,
    token_grad_hbm, gate_grad_hbm, up_grad_hbm, down_grad_hbm,
    token_grad, gate_grad, up_grad, down_grad, gate_codes, up_codes, down_codes, gate_scales, up_scales, down_scales,
    acts_in, fetch_buf, w_gu, w_down, mine, other, mate_in, sum_out, sum_in,
    hidden, grad_out, down_out, grad_in, down_in, grad_own, down_own,
    ring_buf, ring_in, side_buf, side_in, last_buf, last_in,
    load_sems, store_sems, send_sems, recv_sems,
):
    dp = lax.axis_index("dp")
    node = lax.axis_index("node")
    z, x, low = dp // 8, (dp // 2) % 4, dp % 2
    chip, core = node // 2, node % 2
    par = x % 2
    mate = node + 1 - 2 * core
    pair = dp + 2 - 4 * par
    side = (x // 2) * 2 + low

    def at_z(step):
        return lax.rem(z + step + 8, 8) * 8 + x * 2 + low

    def at_chip(step):
        return lax.rem(chip + step + 4, 4)

    def at_side(member):
        return z * 8 + (par + 2 * (member // 2)) * 2 + member % 2

    loads = [
        pltpu.make_async_copy(src, dst, load_sems.at[i])
        for i, (src, dst) in enumerate((
            (gate_codes_hbm, gate_codes), (up_codes_hbm, up_codes), (down_codes_hbm, down_codes),
            (gate_scales_hbm, gate_scales), (up_scales_hbm, up_scales), (down_scales_hbm, down_scales),
        ))
    ]
    for load in loads:
        load.start()

    counts = {"send": 0, "recv": 0}

    def fresh(kind, number=1):
        first = counts[kind]
        counts[kind] += number
        return first

    sent = []

    def push(src, dst, recv, to_dp, to_node, when=None):
        copy = pltpu.make_async_remote_copy(
            src_ref=src, dst_ref=dst, send_sem=send_sems.at[fresh("send")], recv_sem=recv_sems.at[recv],
            device_id={"dp": to_dp, "node": to_node}, device_id_type=MESH,
        )
        if when is None:
            copy.start()
        else:
            pl.when(when)(copy.start)
        sent.append((copy, when))

    def landed(dst, recv):
        pltpu.make_async_copy(dst, dst, recv_sems.at[recv]).wait()

    barrier = pltpu.get_barrier_semaphore()

    def greet(to_dp, to_node):
        pl.semaphore_signal(barrier, inc=1, device_id={"dp": to_dp, "node": to_node}, device_id_type=MESH)

    for step in range(1, 8):
        greet(dp, lax.rem(node + step, 8))
    greet(at_z(1), node)
    greet(at_z(-1), node)
    greet(pair, node)
    for step in range(1, 4):
        greet(at_side(lax.rem(side + step, 4)), node)
    def odd_half(where, origin):
        return lax.rem(lax.rem(where - where % 2 - origin + 16, 8) // 4 + where, 2)

    def last_to(block, cut):
        to_chip = lax.rem(chip + odd_half(z, node) + 2 * cut, 4)
        return node * 8 + lax.rem(x + block, 4) * 2 + low, to_chip * 2 + par

    def is_me(where):
        return jnp.logical_and(where[0] == dp, where[1] == node)

    expected = 13

    pl.semaphore_wait(barrier, expected)

    def quarter_rows(quarter):
        return pl.ds(pl.multiple_of(quarter * CUT, 16), CUT)

    def cols_of(to_node):
        return pl.ds(pl.multiple_of(to_node * WIDE, 128), WIDE)

    is_src = core == par
    fetch_recv = [fresh("recv") for _ in range(3)]
    stage_recv = [fresh("recv") for _ in range(3)]
    own_recv = [fresh("recv") for _ in range(2)]
    own_rows = quarter_rows(z // 2)
    far_steps = (2, 1, 3)
    for a, arr in enumerate((tok, cot)):
        here = jnp.logical_and(is_src, z % 2 == a)
        for step in far_steps:
            push(
                arr.at[own_rows, cols_of(at_chip(step) * 2 + 1 - core)], fetch_buf.at[step - 1],
                stage_recv[step - 1], dp, mate, when=here,
            )
        for step in far_steps:
            to_node = at_chip(step) * 2 + core
            push(
                arr.at[own_rows, cols_of(to_node)], acts_in.at[a, chip, own_rows, :],
                fetch_recv[step - 1], dp, to_node, when=here,
            )

    for a, arr in enumerate((tok, cot)):
        push(arr.at[:, cols_of(mate)], acts_in.at[a, chip], own_recv[a], dp, mate, when=is_src)

        @pl.when(is_src)
        def _(a=a, arr=arr):
            pltpu.make_async_copy(
                arr.at[:, cols_of(node)], acts_in.at[a, chip], recv_sems.at[own_recv[a]]
            ).start()

    not_src = jnp.logical_not(is_src)
    for step in far_steps:
        pl.when(not_src)(lambda step=step: landed(fetch_buf.at[step - 1], stage_recv[step - 1]))
        push(
            fetch_buf.at[step - 1], acts_in.at[z % 2, chip, own_rows, :], fetch_recv[step - 1],
            dp, at_chip(step) * 2 + core, when=not_src,
        )

    for load in loads:
        load.wait()
    eye = lax.broadcasted_iota(jnp.int32, (HID, HID), 0) == lax.broadcasted_iota(jnp.int32, (HID, HID), 1)
    for b in range(WIDE // QB):
        rows = slice(b * QB, (b + 1) * QB)
        line = pl.ds(node * (WIDE // QB) + b, 1)
        w_gu[0, rows, 0:HID] = (gate_codes[rows, :].astype(F32) * gate_scales[line, :]).astype(BF)
        w_gu[0, rows, HID:] = (up_codes[rows, :].astype(F32) * up_scales[line, :]).astype(BF)
        column = jnp.sum(jnp.where(eye, down_scales[line, :], 0.0), axis=1, keepdims=True)
        w_down[0, :, rows] = (down_codes[:, rows].astype(F32) * column).astype(BF)

    w_recv = [fresh("recv") for _ in range(2)]
    push(w_gu.at[0], w_gu.at[1], w_recv[0], pair, node)
    push(w_down.at[0], w_down.at[1], w_recv[1], pair, node)

    up_recv = [[fresh("recv") for _ in range(3)] for _ in range(3)]
    dn_recv = [[fresh("recv") for _ in range(3)] for _ in range(3)]
    far_recv = [fresh("recv") for _ in range(3)]

    def block(turn, step):
        piece = lax.rem(z + turn + 8, 8)
        return acts_in.at[piece % 2, at_chip(-step), quarter_rows(piece // 2), :]

    def relay(turn, step):
        if turn == 0:
            landed(block(0, step), fetch_recv[step - 1])
            push(block(0, step), block(0, step), up_recv[0][step - 1], at_z(1), node)
            push(block(0, step), block(0, step), dn_recv[0][step - 1], at_z(-1), node)
            return
        if turn == 4:
            landed(block(4, step), far_recv[step - 1])
            return
        here = block(-turn, step)
        landed(here, up_recv[turn - 1][step - 1])
        if turn < 3:
            push(here, here, up_recv[turn][step - 1], at_z(1), node)
        elif step != 3:
            push(here, here, far_recv[step - 1], at_z(1), node, when=None if step == 1 else core == 0)
        here = block(turn, step)
        landed(here, dn_recv[turn - 1][step - 1])
        if turn < 3:
            push(here, here, dn_recv[turn][step - 1], at_z(-1), node)
        elif step != 1:
            push(here, here, far_recv[step - 1], at_z(-1), node, when=None if step == 3 else core == 1)

    sign = 1 - 2 * (z % 2)
    quarters = [
        lax.rem(z + first * sign + 8, 8) // 2 for first in (0, -1, 2, -3)
    ]
    mate_recv = [fresh("recv") for _ in range(4)]
    sum_recv = [[fresh("recv") for _ in range(3)] for _ in range(4)]
    hid_recv = [[fresh("recv") for _ in range(3)] for _ in range(4)]
    hid_mate = [[fresh("recv") for _ in range(4)] for _ in range(4)]

    def multiply(s):
        rows = quarter_rows(quarters[s])
        tokens = acts_in[0, :, rows, :].reshape(4 * CUT, WIDE)
        grads = acts_in[1, :, rows, :].reshape(4 * CUT, WIDE)
        for part, store in ((1 - core, other), (core, mine)):
            store[s, :, :, 0 : 2 * HID] = (
                dot_nn(tokens, w_gu[part]).reshape(4, CUT, 2 * HID).astype(store.dtype)
            )
            store[s, :, :, 2 * HID :] = (
                dot_nt(grads, w_down[part]).reshape(4, CUT, HID).astype(store.dtype)
            )
            if store is other:
                push(other.at[s], mate_in.at[s], mate_recv[s], dp, mate)

    def combine(s):
        landed(mate_in.at[s], mate_recv[s])
        for step in far_steps:
            to = at_chip(step)
            sum_out[s, step - 1] = (mine[s, to] + mate_in[s, to].astype(F32)).astype(BF)
            push(
                sum_out.at[s, step - 1], sum_in.at[s, step - 1], sum_recv[s][step - 1],
                dp, to * 2 + core,
            )

    def activate(s):
        full = mine[s, chip] + mate_in[s, chip].astype(F32)
        for i in (0, 2, 1):
            landed(sum_in.at[s, i], sum_recv[s][i])
            full = full + sum_in[s, i].astype(F32)
        rows = quarter_rows(quarters[s])
        gate, upper, d_act = full[:, 0:HID], full[:, HID : 2 * HID], full[:, 2 * HID :]
        sig = jax.nn.sigmoid(gate)
        silu = gate * sig
        hidden[core, chip, rows, 0:HID] = (d_act * upper * sig * (1.0 + gate * (1.0 - sig))).astype(BF)
        hidden[core, chip, rows, HID : 2 * HID] = (d_act * silu).astype(BF)
        hidden[core, chip, rows, 2 * HID :] = (silu * upper).astype(BF)
        own = hidden.at[core, chip, rows]
        for step in far_steps:
            push(own, own, hid_recv[s][step - 1], dp, at_chip(step) * 2 + core)
        push(own, own, hid_mate[s][0], dp, mate)

    def forward_hidden(s):
        rows = quarter_rows(quarters[s])
        for step in (1, 3, 2):
            here = hidden.at[core, at_chip(-step), rows]
            landed(here, hid_recv[s][step - 1])
            push(here, here, hid_mate[s][step], dp, mate)

    def finish_hidden(s):
        rows = quarter_rows(quarters[s])
        for step in range(4):
            landed(hidden.at[1 - core, at_chip(-step), rows], hid_mate[s][step])

    ring_slot = {-3: 0, 3: 1, -2: 2, 2: 3, -1: 4, 1: 5, 0: 6}
    ring_recv = [[fresh("recv") for _ in range(2)] for _ in range(8)]
    buf_slot = {4: 0, 3: 1, -3: 2, 2: 3, -2: 4, 1: 5, -1: 6}
    pairs = ((4, -3), (2, 3), (-2, -1), (0, 1))

    def cut_rows(cut):
        return slice(cut * CUT, (cut + 1) * CUT)

    def token_terms(s, i):
        rows = quarter_rows(quarters[s])
        half = odd_half(lax.rem(2 * quarters[s] + 4, 8) + lax.rem(i + z, 2), node)
        total = None
        for part in range(2):
            data = jnp.concatenate(
                [hidden[part, lax.rem(chip + half + 2 * cut, 4), rows, 0 : 2 * HID] for cut in range(2)], axis=0
            )
            term = dot_nt(data, w_gu[part])
            total = term if total is None else total + term
        return total

    def chain(far):
        s, i = [(s, pair.index(far)) for s, pair in enumerate(pairs) if far in pair][0]
        terms = token_terms(s, i)
        if far == 0:
            return terms
        way = 1 if far > 0 else -1
        buf = buf_slot[far]
        for cut in range(2):
            rows = cut_rows(cut)
            value = terms[rows]
            if abs(far) < 3 or far == (-3, 3)[cut]:
                slot = ring_slot[far]
                landed(ring_in.at[slot, rows], ring_recv[slot][cut])
                value = value + ring_in[slot, rows].astype(F32)
            ring_buf[buf, rows] = value.astype(BF)
            if far == 4:
                to, slot = sign * (1 - 2 * cut), (0, 1)[cut]
            else:
                to, slot = sign * way, 7 if far == -1 else ring_slot[-(far - way)]
            push(ring_buf.at[buf, rows], ring_in.at[slot, rows], ring_recv[slot][cut], at_z(to), node)
        return None

    for step in (1, 3, 2):
        relay(0, step)
    relay(1, 1)
    relay(1, 3)
    for a in range(2):
        landed(acts_in.at[a, chip], own_recv[a])
    relay(1, 2)
    landed(w_gu.at[1], w_recv[0])
    landed(w_down.at[1], w_recv[1])
    multiply(0)
    relay(2, 1)
    combine(0)
    relay(2, 3)
    relay(2, 2)
    multiply(1)
    relay(3, 1)
    combine(1)
    relay(3, 3)
    relay(3, 2)
    multiply(2)
    activate(0)
    relay(4, 1)
    combine(2)
    relay(4, 3)
    relay(4, 2)
    multiply(3)
    activate(1)
    combine(3)
    forward_hidden(0)
    activate(2)
    finish_hidden(0)
    forward_hidden(1)
    chain(4)
    activate(3)
    finish_hidden(1)
    forward_hidden(2)
    chain(-3)
    chain(3)
    finish_hidden(2)
    forward_hidden(3)
    chain(2)
    chain(-2)
    finish_hidden(3)
    chain(-1)
    chain(1)

    def cols(b):
        return slice(b * HID, (b + 1) * HID)

    def weight_grads(part):
        tokens = acts_in[0].reshape(4 * ROWS, WIDE)
        grads = acts_in[1].reshape(4 * ROWS, WIDE)
        back = hidden[part].reshape(4 * ROWS, 3 * HID)
        return dot_tn(tokens, back[:, 0 : 2 * HID]), dot_tn(back[:, 2 * HID :], grads)

    first, second = weight_grads(1)
    grad_out[...] = first.astype(BF)
    down_out[...] = second.astype(BF)
    grad_recv = [fresh("recv") for _ in range(3)]
    push(down_out, down_in, grad_recv[0], pair, node)

    terms = chain(0)

    first, second = weight_grads(0)
    grad_own[...] = first
    down_own[...] = second

    for slot in (7, 6):
        for cut in range(2):
            landed(ring_in.at[slot, cut_rows(cut)], ring_recv[slot][cut])
    terms = terms + ring_in[6].astype(F32) + ring_in[7].astype(F32)
    for i in range(8):
        turn = lax.rem(i // 2 - par + 4, 4)
        member, b = (turn // 2) * 2 + i % 2, lax.rem(turn, 2)
        side_buf[member, b, :, 0:N_COLS] = terms[:, i * N_COLS : (i + 1) * N_COLS].astype(BF)
        side_buf[member, b, :, N_COLS:] = jnp.zeros((96, 128 - N_COLS), BF)

    side_recv = [fresh("recv") for _ in range(3)]
    for step in range(1, 4):
        to = lax.rem(side + step, 4)
        push(side_buf.at[to], side_in.at[step - 1], side_recv[step - 1], at_side(to), node)
    for b in range(2):
        push(grad_out.at[:, cols(b)], grad_in.at[:, cols(b)], grad_recv[1 + b], pair, node)
    total = side_buf[side].astype(F32)
    for step in range(1, 4):
        landed(side_in.at[step - 1], side_recv[step - 1])
        total = total + side_in[step - 1].astype(F32)
    last_buf[...] = total.astype(BF)

    last_recv = fresh("recv", 4)
    quarter = lax.rem(z // 2 + 2, 4)
    for b in range(2):
        for cut in range(2):
            where = last_to(b, cut)
            src, dst, recv = last_buf.at[b, cut_rows(cut)], last_in.at[quarter], last_recv + quarter
            push(src, dst, recv, *where, when=jnp.logical_not(is_me(where)))

            @pl.when(is_me(where))
            def _(src=src, dst=dst, recv=recv):
                pltpu.make_async_copy(src, dst, recv_sems.at[recv]).start()

    landed(down_in, grad_recv[0])
    for b in range(2):
        landed(grad_in.at[:, cols(b)], grad_recv[1 + b])
    gate_grad[...] = (grad_own[:, 0:HID] + grad_in[:, 0:HID].astype(F32)).astype(BF)
    up_grad[...] = (grad_own[:, HID:] + grad_in[:, HID:].astype(F32)).astype(BF)
    down_grad[...] = (down_own[...] + down_in[...].astype(F32)).astype(BF)
    stores = [
        pltpu.make_async_copy(src, dst, store_sems.at[i])
        for i, (src, dst) in enumerate((
            (gate_grad, gate_grad_hbm), (up_grad, up_grad_hbm), (down_grad, down_grad_hbm),
            (token_grad, token_grad_hbm),
        ))
    ]
    for store in stores[:3]:
        store.start()

    for i in range(4):
        landed(last_in.at[i], last_recv + i)
    token_grad[...] = jnp.transpose(last_in[...].reshape(ROWS, 128).astype(F32))[0:N_COLS, :].astype(BF)
    stores[3].start()

    assert max(counts.values()) <= SEMS

    for copy, when in sent:
        if when is None:
            copy.wait_send()
        else:
            pl.when(when)(copy.wait_send)
    for store in stores:
        store.wait()


def write_out(*refs):
    for src, dst in zip(refs[:4], refs[4:]):
        dst[...] = src[...]


def body(tok, cot, gate_codes, up_codes, down_codes, gate_scales, up_scales, down_scales):
    hbm = pl.BlockSpec(memory_space=pltpu.HBM)
    outs = (
        jax.ShapeDtypeStruct((N_COLS, ROWS), BF),
        jax.ShapeDtypeStruct((WIDE, HID), BF),
        jax.ShapeDtypeStruct((WIDE, HID), BF),
        jax.ShapeDtypeStruct((HID, WIDE), BF),
    )
    results = pl.pallas_call(
        kernel,
        out_shape=outs,
        in_specs=[hbm] * 8,
        out_specs=(hbm,) * 4,
        scratch_shapes=[
            pltpu.VMEM((N_COLS, ROWS), BF),
            pltpu.VMEM((WIDE, HID), BF),
            pltpu.VMEM((WIDE, HID), BF),
            pltpu.VMEM((HID, WIDE), BF),
            pltpu.VMEM((WIDE, HID), BF),
            pltpu.VMEM((WIDE, HID), BF),
            pltpu.VMEM((HID, WIDE), BF),
            pltpu.VMEM((40, HID), F32),
            pltpu.VMEM((40, HID), F32),
            pltpu.VMEM((40, HID), F32),
            pltpu.VMEM((2, 4, ROWS, WIDE), BF),
            pltpu.VMEM((3, CUT, WIDE), BF),
            pltpu.VMEM((2, WIDE, 2 * HID), BF),
            pltpu.VMEM((2, HID, WIDE), BF),
            pltpu.VMEM((4, 4, CUT, 3 * HID), F32),
            pltpu.VMEM((4, 4, CUT, 3 * HID), BF),
            pltpu.VMEM((4, 4, CUT, 3 * HID), BF),
            pltpu.VMEM((4, 3, CUT, 3 * HID), BF),
            pltpu.VMEM((4, 3, CUT, 3 * HID), BF),
            pltpu.VMEM((2, 4, ROWS, 3 * HID), BF),
            pltpu.VMEM((WIDE, 2 * HID), BF),
            pltpu.VMEM((HID, WIDE), BF),
            pltpu.VMEM((WIDE, 2 * HID), BF),
            pltpu.VMEM((HID, WIDE), BF),
            pltpu.VMEM((WIDE, 2 * HID), F32),
            pltpu.VMEM((HID, WIDE), F32),
            pltpu.VMEM((7, 96, WIDE), BF),
            pltpu.VMEM((8, 96, WIDE), BF),
            pltpu.VMEM((4, 2, 96, 128), BF),
            pltpu.VMEM((3, 2, 96, 128), BF),
            pltpu.VMEM((2, 96, 128), BF),
            pltpu.VMEM((4, CUT, 128), BF),
            pltpu.SemaphoreType.DMA((6,)),
            pltpu.SemaphoreType.DMA((4,)),
            pltpu.SemaphoreType.DMA((SEMS,)),
            pltpu.SemaphoreType.DMA((SEMS,)),
        ],
        compiler_params=pltpu.CompilerParams(
            collective_id=0, has_side_effects=True, vmem_limit_bytes=VMEM_BYTES
        ),
        cost_estimate=pl.CostEstimate(flops=2_100_000_000, bytes_accessed=5_000_000, transcendentals=25_000),
    )(tok, cot, gate_codes, up_codes, down_codes, gate_scales, up_scales, down_scales.T)
    results = pl.pallas_call(
        write_out,
        out_shape=outs,
        compiler_params=pltpu.CompilerParams(vmem_limit_bytes=VMEM_BYTES),
    )(*results)
    return (results[0].T,) + tuple(results[1:])


def solution(mesh):
    return jax.shard_map(
        body,
        mesh=mesh,
        in_specs=(
            P("node", None),
            P("node", None),
            P("node", "dp"),
            P("node", "dp"),
            P("dp", "node"),
            P(None, "dp"),
            P(None, "dp"),
            P("dp", None),
        ),
        out_specs=(P("node", "dp"), P("node", "dp"), P("node", "dp"), P("dp", "node")),
        check_vma=False,
    )
```

```python
import jax
import jax.numpy as jnp
from jax import lax
from jax.experimental import pallas as pl
from jax.experimental.pallas import tpu as pltpu
from jax.sharding import PartitionSpec as P

BF = jnp.bfloat16
F32 = jnp.float32
MESH = pl.DeviceIdType.MESH

ROWS = 192
WIDE = 640
HID = 128
QB = 128
CUT = 48
VMEM_BYTES = 60 * 1024 * 1024
SEMS = 160
RELAYED = (0, 1, 2, 3)
N_COLS = 80


def dot_nn(a, b):
    return lax.dot_general(a, b, (((1,), (0,)), ((), ())), preferred_element_type=F32)


def dot_nt(a, b):
    return lax.dot_general(a, b, (((1,), (1,)), ((), ())), preferred_element_type=F32)


def dot_tn(a, b):
    return lax.dot_general(a, b, (((0,), (0,)), ((), ())), preferred_element_type=F32)


def kernel(
    tok, cot, gate_codes_hbm, up_codes_hbm, down_codes_hbm, gate_scales_hbm, up_scales_hbm, down_scales_hbm,
    token_grad_hbm, gate_grad_hbm, up_grad_hbm, down_grad_hbm,
    token_grad, gate_grad, up_grad, down_grad, gate_codes, up_codes, down_codes, gate_scales, up_scales, down_scales,
    acts_in, fetch_buf, w_gu, w_down, mine, other, mate_in, sum_out, sum_in,
    hidden, grad_out, down_out, grad_in, down_in, grad_own, down_own,
    ring_buf, ring_in, side_buf, side_in, last_buf, last_in,
    load_sems, store_sems, send_sems, recv_sems,
):
    dp = lax.axis_index("dp")
    node = lax.axis_index("node")
    z, x, low = dp // 8, (dp // 2) % 4, dp % 2
    chip, core = node // 2, node % 2
    par = x % 2
    mate = node + 1 - 2 * core
    pair = dp + 2 - 4 * par
    side = (x // 2) * 2 + low

    def at_z(step):
        return lax.rem(z + step + 8, 8) * 8 + x * 2 + low

    def at_chip(step):
        return lax.rem(chip + step + 4, 4)

    def at_side(member):
        return z * 8 + (par + 2 * (member // 2)) * 2 + member % 2

    loads = [
        pltpu.make_async_copy(src, dst, load_sems.at[i])
        for i, (src, dst) in enumerate((
            (gate_codes_hbm, gate_codes), (up_codes_hbm, up_codes), (down_codes_hbm, down_codes),
            (gate_scales_hbm, gate_scales), (up_scales_hbm, up_scales), (down_scales_hbm, down_scales),
        ))
    ]
    for load in loads:
        load.start()

    counts = {"send": 0, "recv": 0}

    def fresh(kind, number=1):
        first = counts[kind]
        counts[kind] += number
        return first

    sent = []

    def push(src, dst, recv, to_dp, to_node, when=None):
        copy = pltpu.make_async_remote_copy(
            src_ref=src, dst_ref=dst, send_sem=send_sems.at[fresh("send")], recv_sem=recv_sems.at[recv],
            device_id={"dp": to_dp, "node": to_node}, device_id_type=MESH,
        )
        if when is None:
            copy.start()
        else:
            pl.when(when)(copy.start)
        sent.append((copy, when))

    def landed(dst, recv):
        pltpu.make_async_copy(dst, dst, recv_sems.at[recv]).wait()

    barrier = pltpu.get_barrier_semaphore()

    def greet(to_dp, to_node):
        pl.semaphore_signal(barrier, inc=1, device_id={"dp": to_dp, "node": to_node}, device_id_type=MESH)

    for step in range(1, 8):
        greet(dp, lax.rem(node + step, 8))
    greet(at_z(1), node)
    greet(at_z(-1), node)
    greet(pair, node)
    for step in range(1, 4):
        greet(at_side(lax.rem(side + step, 4)), node)
    def odd_half(where, origin):
        return lax.rem(lax.rem(where - where % 2 - origin + 16, 8) // 4 + where, 2)

    def last_to(block, cut):
        to_chip = lax.rem(chip + odd_half(z, node) + 2 * cut, 4)
        return node * 8 + lax.rem(x + block, 4) * 2 + low, to_chip * 2 + par

    def is_me(where):
        return jnp.logical_and(where[0] == dp, where[1] == node)

    expected = 13

    pl.semaphore_wait(barrier, expected)

    def quarter_rows(quarter):
        return pl.ds(pl.multiple_of(quarter * CUT, 16), CUT)

    def cols_of(to_node):
        return pl.ds(pl.multiple_of(to_node * WIDE, 128), WIDE)

    is_src = core == par
    fetch_recv = [fresh("recv") for _ in range(3)]
    stage_recv = [fresh("recv") for _ in range(3)]
    own_recv = [fresh("recv") for _ in range(2)]
    own_rows = quarter_rows(z // 2)
    far_steps = (2, 1, 3)
    for a, arr in enumerate((tok, cot)):
        here = jnp.logical_and(is_src, z % 2 == a)
        for step in far_steps:
            push(
                arr.at[own_rows, cols_of(at_chip(step) * 2 + 1 - core)], fetch_buf.at[step - 1],
                stage_recv[step - 1], dp, mate, when=here,
            )
        for step in far_steps:
            to_node = at_chip(step) * 2 + core
            push(
                arr.at[own_rows, cols_of(to_node)], acts_in.at[a, chip, own_rows, :],
                fetch_recv[step - 1], dp, to_node, when=here,
            )

    for a, arr in enumerate((tok, cot)):
        push(arr.at[:, cols_of(mate)], acts_in.at[a, chip], own_recv[a], dp, mate, when=is_src)

        @pl.when(is_src)
        def _(a=a, arr=arr):
            pltpu.make_async_copy(
                arr.at[:, cols_of(node)], acts_in.at[a, chip], recv_sems.at[own_recv[a]]
            ).start()

    not_src = jnp.logical_not(is_src)
    for step in far_steps:
        pl.when(not_src)(lambda step=step: landed(fetch_buf.at[step - 1], stage_recv[step - 1]))
        push(
            fetch_buf.at[step - 1], acts_in.at[z % 2, chip, own_rows, :], fetch_recv[step - 1],
            dp, at_chip(step) * 2 + core, when=not_src,
        )

    for load in loads:
        load.wait()
    eye = lax.broadcasted_iota(jnp.int32, (HID, HID), 0) == lax.broadcasted_iota(jnp.int32, (HID, HID), 1)
    for b in range(WIDE // QB):
        rows = slice(b * QB, (b + 1) * QB)
        line = pl.ds(node * (WIDE // QB) + b, 1)
        w_gu[0, rows, 0:HID] = (gate_codes[rows, :].astype(F32) * gate_scales[line, :]).astype(BF)
        w_gu[0, rows, HID:] = (up_codes[rows, :].astype(F32) * up_scales[line, :]).astype(BF)
        column = jnp.sum(jnp.where(eye, down_scales[line, :], 0.0), axis=1, keepdims=True)
        w_down[0, :, rows] = (down_codes[:, rows].astype(F32) * column).astype(BF)

    w_recv = [fresh("recv") for _ in range(2)]
    push(w_gu.at[0], w_gu.at[1], w_recv[0], pair, node)
    push(w_down.at[0], w_down.at[1], w_recv[1], pair, node)

    up_recv = [[fresh("recv") for _ in range(3)] for _ in range(3)]
    dn_recv = [[fresh("recv") for _ in range(3)] for _ in range(3)]
    far_recv = [fresh("recv") for _ in range(3)]

    def block(turn, step):
        piece = lax.rem(z + turn + 8, 8)
        return acts_in.at[piece % 2, at_chip(-step), quarter_rows(piece // 2), :]

    def relay(turn, step):
        if turn == 0:
            landed(block(0, step), fetch_recv[step - 1])
            push(block(0, step), block(0, step), up_recv[0][step - 1], at_z(1), node)
            push(block(0, step), block(0, step), dn_recv[0][step - 1], at_z(-1), node)
            return
        if turn == 4:
            landed(block(4, step), far_recv[step - 1])
            return
        here = block(-turn, step)
        landed(here, up_recv[turn - 1][step - 1])
        if turn < 3:
            push(here, here, up_recv[turn][step - 1], at_z(1), node)
        elif step != 3:
            push(here, here, far_recv[step - 1], at_z(1), node, when=None if step == 1 else core == 0)
        here = block(turn, step)
        landed(here, dn_recv[turn - 1][step - 1])
        if turn < 3:
            push(here, here, dn_recv[turn][step - 1], at_z(-1), node)
        elif step != 1:
            push(here, here, far_recv[step - 1], at_z(-1), node, when=None if step == 3 else core == 1)

    sign = 1 - 2 * (z % 2)
    quarters = [
        lax.rem(z + first * sign + 8, 8) // 2 for first in (0, -1, 2, -3)
    ]
    mate_recv = [fresh("recv") for _ in range(4)]
    sum_recv = [[fresh("recv") for _ in range(3)] for _ in range(4)]
    hid_recv = [[fresh("recv") for _ in range(3)] for _ in range(4)]
    hid_far = [[fresh("recv") for _ in range(3)] for _ in range(4)]
    ways = (1, 1 - 2 * core, -1)

    def cols(b):
        return slice(b * HID, (b + 1) * HID)

    hid_mate = [[fresh("recv") for _ in range(4)] for _ in range(4)]

    def multiply(s):
        rows = quarter_rows(quarters[s])
        tokens = acts_in[0, :, rows, :].reshape(4 * CUT, WIDE)
        grads = acts_in[1, :, rows, :].reshape(4 * CUT, WIDE)
        for part, store in ((1 - core, other), (core, mine)):
            store[s, :, :, 0 : 2 * HID] = (
                dot_nn(tokens, w_gu[part]).reshape(4, CUT, 2 * HID).astype(store.dtype)
            )
            store[s, :, :, 2 * HID :] = (
                dot_nt(grads, w_down[part]).reshape(4, CUT, HID).astype(store.dtype)
            )
            if store is other:
                push(other.at[s], mate_in.at[s], mate_recv[s], dp, mate)

    def combine(s):
        landed(mate_in.at[s], mate_recv[s])
        for step in far_steps:
            to = at_chip(step)
            sum_out[s, step - 1] = (mine[s, to] + mate_in[s, to].astype(F32)).astype(BF)
            push(
                sum_out.at[s, step - 1], sum_in.at[s, step - 1], sum_recv[s][step - 1],
                dp, to * 2 + core,
            )

    def activate(s):
        full = mine[s, chip] + mate_in[s, chip].astype(F32)
        for i in (0, 2, 1):
            landed(sum_in.at[s, i], sum_recv[s][i])
            full = full + sum_in[s, i].astype(F32)
        rows = quarter_rows(quarters[s])
        gate, upper, d_act = full[:, 0:HID], full[:, HID : 2 * HID], full[:, 2 * HID :]
        sig = jax.nn.sigmoid(gate)
        silu = gate * sig
        hidden[core, chip, rows, 0:HID] = (d_act * upper * sig * (1.0 + gate * (1.0 - sig))).astype(BF)
        hidden[core, chip, rows, HID : 2 * HID] = (d_act * silu).astype(BF)
        hidden[core, chip, rows, 2 * HID :] = (silu * upper).astype(BF)
        own = hidden.at[core, chip, rows]
        for step in (1, 3) if s in RELAYED else far_steps:
            push(own, own, hid_recv[s][step - 1], dp, at_chip(step) * 2 + core)
        push(own, own, hid_mate[s][0], dp, mate)

    def forward_hidden(s):
        rows = quarter_rows(quarters[s])
        for step in (1, 3) if s in RELAYED else (1, 3, 2):
            here = hidden.at[core, at_chip(-step), rows]
            landed(here, hid_recv[s][step - 1])
            push(here, here, hid_mate[s][step], dp, mate)
        if s in RELAYED:
            for b in range(3):
                here = hidden.at[core, at_chip(-ways[b]), rows, cols(b)]
                push(here, here, hid_far[s][b], dp, at_chip(ways[b]) * 2 + core)

    def last_hidden(s):
        rows = quarter_rows(quarters[s])
        for b in range(3):
            landed(hidden.at[core, at_chip(2), rows, cols(b)], hid_far[s][b])
        here = hidden.at[core, at_chip(2), rows]
        push(here, here, hid_mate[s][2], dp, mate)

    def finish_hidden(s):
        rows = quarter_rows(quarters[s])
        for step in range(4):
            landed(hidden.at[1 - core, at_chip(-step), rows], hid_mate[s][step])

    ring_slot = {-3: 0, 3: 1, -2: 2, 2: 3, -1: 4, 1: 5, 0: 6}
    ring_recv = [[fresh("recv") for _ in range(2)] for _ in range(8)]
    buf_slot = {4: 0, 3: 1, -3: 2, 2: 3, -2: 4, 1: 5, -1: 6}
    pairs = ((4, -3), (2, 3), (-2, -1), (0, 1))

    def cut_rows(cut):
        return slice(cut * CUT, (cut + 1) * CUT)

    def token_terms(s, i):
        rows = quarter_rows(quarters[s])
        half = odd_half(lax.rem(2 * quarters[s] + 4, 8) + lax.rem(i + z, 2), node)
        total = None
        for part in range(2):
            data = jnp.concatenate(
                [hidden[part, lax.rem(chip + half + 2 * cut, 4), rows, 0 : 2 * HID] for cut in range(2)], axis=0
            )
            term = dot_nt(data, w_gu[part])
            total = term if total is None else total + term
        return total

    def chain(far):
        s, i = [(s, pair.index(far)) for s, pair in enumerate(pairs) if far in pair][0]
        terms = token_terms(s, i)
        if far == 0:
            return terms
        way = 1 if far > 0 else -1
        buf = buf_slot[far]
        for cut in range(2):
            rows = cut_rows(cut)
            value = terms[rows]
            if abs(far) < 3 or far == (-3, 3)[cut]:
                slot = ring_slot[far]
                landed(ring_in.at[slot, rows], ring_recv[slot][cut])
                value = value + ring_in[slot, rows].astype(F32)
            ring_buf[buf, rows] = value.astype(BF)
            if far == 4:
                to, slot = sign * (1 - 2 * cut), (0, 1)[cut]
            else:
                to, slot = sign * way, 7 if far == -1 else ring_slot[-(far - way)]
            push(ring_buf.at[buf, rows], ring_in.at[slot, rows], ring_recv[slot][cut], at_z(to), node)
        return None

    for step in (1, 3, 2):
        relay(0, step)
    relay(1, 1)
    relay(1, 3)
    for a in range(2):
        landed(acts_in.at[a, chip], own_recv[a])
    relay(1, 2)
    landed(w_gu.at[1], w_recv[0])
    landed(w_down.at[1], w_recv[1])
    multiply(0)
    relay(2, 1)
    combine(0)
    relay(2, 3)
    relay(2, 2)
    multiply(1)
    relay(3, 1)
    combine(1)
    relay(3, 3)
    relay(3, 2)
    multiply(2)
    activate(0)
    relay(4, 1)
    combine(2)
    relay(4, 3)
    relay(4, 2)
    multiply(3)
    activate(1)
    combine(3)
    forward_hidden(0)
    activate(2)
    forward_hidden(1)
    last_hidden(0)
    activate(3)
    finish_hidden(0)
    chain(4)
    forward_hidden(2)
    last_hidden(1)
    finish_hidden(1)
    chain(-3)
    chain(3)
    last_hidden(2)
    forward_hidden(3)
    finish_hidden(2)
    last_hidden(3)
    chain(2)
    chain(-2)
    finish_hidden(3)
    chain(-1)
    chain(1)

    def weight_grads(part):
        tokens = acts_in[0].reshape(4 * ROWS, WIDE)
        grads = acts_in[1].reshape(4 * ROWS, WIDE)
        back = hidden[part].reshape(4 * ROWS, 3 * HID)
        return dot_tn(tokens, back[:, 0 : 2 * HID]), dot_tn(back[:, 2 * HID :], grads)

    first, second = weight_grads(1)
    grad_out[...] = first.astype(BF)
    down_out[...] = second.astype(BF)
    grad_recv = [fresh("recv") for _ in range(3)]
    push(down_out, down_in, grad_recv[0], pair, node)

    terms = chain(0)

    first, second = weight_grads(0)
    grad_own[...] = first
    down_own[...] = second

    for slot in (7, 6):
        for cut in range(2):
            landed(ring_in.at[slot, cut_rows(cut)], ring_recv[slot][cut])
    terms = terms + ring_in[6].astype(F32) + ring_in[7].astype(F32)
    for i in range(8):
        turn = lax.rem(i // 2 - par + 4, 4)
        member, b = (turn // 2) * 2 + i % 2, lax.rem(turn, 2)
        side_buf[member, b, :, 0:N_COLS] = terms[:, i * N_COLS : (i + 1) * N_COLS].astype(BF)
        side_buf[member, b, :, N_COLS:] = jnp.zeros((96, 128 - N_COLS), BF)

    side_recv = [fresh("recv") for _ in range(3)]
    for step in range(1, 4):
        to = lax.rem(side + step, 4)
        push(side_buf.at[to], side_in.at[step - 1], side_recv[step - 1], at_side(to), node)
    for b in range(2):
        push(grad_out.at[:, cols(b)], grad_in.at[:, cols(b)], grad_recv[1 + b], pair, node)
    total = side_buf[side].astype(F32)
    for step in range(1, 4):
        landed(side_in.at[step - 1], side_recv[step - 1])
        total = total + side_in[step - 1].astype(F32)
    last_buf[...] = total.astype(BF)

    last_recv = fresh("recv", 4)
    quarter = lax.rem(z // 2 + 2, 4)
    for b in range(2):
        for cut in range(2):
            where = last_to(b, cut)
            src, dst, recv = last_buf.at[b, cut_rows(cut)], last_in.at[quarter], last_recv + quarter
            push(src, dst, recv, *where, when=jnp.logical_not(is_me(where)))

            @pl.when(is_me(where))
            def _(src=src, dst=dst, recv=recv):
                pltpu.make_async_copy(src, dst, recv_sems.at[recv]).start()

    landed(down_in, grad_recv[0])
    for b in range(2):
        landed(grad_in.at[:, cols(b)], grad_recv[1 + b])
    gate_grad[...] = (grad_own[:, 0:HID] + grad_in[:, 0:HID].astype(F32)).astype(BF)
    up_grad[...] = (grad_own[:, HID:] + grad_in[:, HID:].astype(F32)).astype(BF)
    down_grad[...] = (down_own[...] + down_in[...].astype(F32)).astype(BF)
    stores = [
        pltpu.make_async_copy(src, dst, store_sems.at[i])
        for i, (src, dst) in enumerate((
            (gate_grad, gate_grad_hbm), (up_grad, up_grad_hbm), (down_grad, down_grad_hbm),
            (token_grad, token_grad_hbm),
        ))
    ]
    for store in stores[:3]:
        store.start()

    for i in range(4):
        landed(last_in.at[i], last_recv + i)
    token_grad[...] = jnp.transpose(last_in[...].reshape(ROWS, 128).astype(F32))[0:N_COLS, :].astype(BF)
    stores[3].start()

    assert max(counts.values()) <= SEMS

    for copy, when in sent:
        if when is None:
            copy.wait_send()
        else:
            pl.when(when)(copy.wait_send)
    for store in stores:
        store.wait()


def write_out(*refs):
    for src, dst in zip(refs[:4], refs[4:]):
        dst[...] = src[...]


def body(tok, cot, gate_codes, up_codes, down_codes, gate_scales, up_scales, down_scales):
    hbm = pl.BlockSpec(memory_space=pltpu.HBM)
    outs = (
        jax.ShapeDtypeStruct((N_COLS, ROWS), BF),
        jax.ShapeDtypeStruct((WIDE, HID), BF),
        jax.ShapeDtypeStruct((WIDE, HID), BF),
        jax.ShapeDtypeStruct((HID, WIDE), BF),
    )
    results = pl.pallas_call(
        kernel,
        out_shape=outs,
        in_specs=[hbm] * 8,
        out_specs=(hbm,) * 4,
        scratch_shapes=[
            pltpu.VMEM((N_COLS, ROWS), BF),
            pltpu.VMEM((WIDE, HID), BF),
            pltpu.VMEM((WIDE, HID), BF),
            pltpu.VMEM((HID, WIDE), BF),
            pltpu.VMEM((WIDE, HID), BF),
            pltpu.VMEM((WIDE, HID), BF),
            pltpu.VMEM((HID, WIDE), BF),
            pltpu.VMEM((40, HID), F32),
            pltpu.VMEM((40, HID), F32),
            pltpu.VMEM((40, HID), F32),
            pltpu.VMEM((2, 4, ROWS, WIDE), BF),
            pltpu.VMEM((3, CUT, WIDE), BF),
            pltpu.VMEM((2, WIDE, 2 * HID), BF),
            pltpu.VMEM((2, HID, WIDE), BF),
            pltpu.VMEM((4, 4, CUT, 3 * HID), F32),
            pltpu.VMEM((4, 4, CUT, 3 * HID), BF),
            pltpu.VMEM((4, 4, CUT, 3 * HID), BF),
            pltpu.VMEM((4, 3, CUT, 3 * HID), BF),
            pltpu.VMEM((4, 3, CUT, 3 * HID), BF),
            pltpu.VMEM((2, 4, ROWS, 3 * HID), BF),
            pltpu.VMEM((WIDE, 2 * HID), BF),
            pltpu.VMEM((HID, WIDE), BF),
            pltpu.VMEM((WIDE, 2 * HID), BF),
            pltpu.VMEM((HID, WIDE), BF),
            pltpu.VMEM((WIDE, 2 * HID), F32),
            pltpu.VMEM((HID, WIDE), F32),
            pltpu.VMEM((7, 96, WIDE), BF),
            pltpu.VMEM((8, 96, WIDE), BF),
            pltpu.VMEM((4, 2, 96, 128), BF),
            pltpu.VMEM((3, 2, 96, 128), BF),
            pltpu.VMEM((2, 96, 128), BF),
            pltpu.VMEM((4, CUT, 128), BF),
            pltpu.SemaphoreType.DMA((6,)),
            pltpu.SemaphoreType.DMA((4,)),
            pltpu.SemaphoreType.DMA((SEMS,)),
            pltpu.SemaphoreType.DMA((SEMS,)),
        ],
        compiler_params=pltpu.CompilerParams(
            collective_id=0, has_side_effects=True, vmem_limit_bytes=VMEM_BYTES
        ),
        cost_estimate=pl.CostEstimate(flops=2_100_000_000, bytes_accessed=5_000_000, transcendentals=25_000),
    )(tok, cot, gate_codes, up_codes, down_codes, gate_scales, up_scales, down_scales.T)
    results = pl.pallas_call(
        write_out,
        out_shape=outs,
        compiler_params=pltpu.CompilerParams(vmem_limit_bytes=VMEM_BYTES),
    )(*results)
    return (results[0].T,) + tuple(results[1:])


def solution(mesh):
    return jax.shard_map(
        body,
        mesh=mesh,
        in_specs=(
            P("node", None),
            P("node", None),
            P("node", "dp"),
            P("node", "dp"),
            P("dp", "node"),
            P(None, "dp"),
            P(None, "dp"),
            P("dp", None),
        ),
        out_specs=(P("node", "dp"), P("node", "dp"), P("node", "dp"), P("dp", "node")),
        check_vma=False,
    )
```

```python
import jax
import jax.numpy as jnp
from jax import lax
from jax.experimental import pallas as pl
from jax.experimental.pallas import tpu as pltpu
from jax.sharding import PartitionSpec as P

BF = jnp.bfloat16
F32 = jnp.float32
MESH = pl.DeviceIdType.MESH

ROWS = 192
WIDE = 640
HID = 128
QB = 128
CUT = 48
VMEM_BYTES = 60 * 1024 * 1024
SEMS = 160
RELAYED = (0, 1, 2, 3)
N_COLS = 80


def dot_nn(a, b):
    return lax.dot_general(a, b, (((1,), (0,)), ((), ())), preferred_element_type=F32)


def dot_nt(a, b):
    return lax.dot_general(a, b, (((1,), (1,)), ((), ())), preferred_element_type=F32)


def dot_tn(a, b):
    return lax.dot_general(a, b, (((0,), (0,)), ((), ())), preferred_element_type=F32)


def kernel(
    tok, cot, gate_codes_hbm, up_codes_hbm, down_codes_hbm, gate_scales_hbm, up_scales_hbm, down_scales_hbm,
    token_grad_hbm, gate_grad_hbm, up_grad_hbm, down_grad_hbm,
    token_grad, gate_grad, up_grad, down_grad, gate_codes, up_codes, down_codes, gate_scales, up_scales, down_scales,
    acts_in, fetch_buf, w_gu, w_down, mine, other, mate_in, sum_out, sum_in,
    hidden, grad_out, down_out, grad_in, down_in, grad_own, down_own,
    ring_buf, ring_in, side_buf, side_in, last_buf, last_in,
    load_sems, store_sems, send_sems, recv_sems,
):
    dp = lax.axis_index("dp")
    node = lax.axis_index("node")
    z, x, low = dp // 8, (dp // 2) % 4, dp % 2
    chip, core = node // 2, node % 2
    par = x % 2
    mate = node + 1 - 2 * core
    pair = dp + 2 - 4 * par
    side = (x // 2) * 2 + low

    def at_z(step):
        return lax.rem(z + step + 8, 8) * 8 + x * 2 + low

    def at_chip(step):
        return lax.rem(chip + step + 4, 4)

    def at_side(member):
        return z * 8 + (par + 2 * (member // 2)) * 2 + member % 2

    loads = [
        pltpu.make_async_copy(src, dst, load_sems.at[i])
        for i, (src, dst) in enumerate((
            (gate_codes_hbm, gate_codes), (up_codes_hbm, up_codes), (down_codes_hbm, down_codes),
            (gate_scales_hbm, gate_scales), (up_scales_hbm, up_scales), (down_scales_hbm, down_scales),
        ))
    ]
    for load in loads:
        load.start()

    counts = {"send": 0, "recv": 0}

    def fresh(kind, number=1):
        first = counts[kind]
        counts[kind] += number
        return first

    sent = []

    def push(src, dst, recv, to_dp, to_node, when=None):
        copy = pltpu.make_async_remote_copy(
            src_ref=src, dst_ref=dst, send_sem=send_sems.at[fresh("send")], recv_sem=recv_sems.at[recv],
            device_id={"dp": to_dp, "node": to_node}, device_id_type=MESH,
        )
        if when is None:
            copy.start()
        else:
            pl.when(when)(copy.start)
        sent.append((copy, when))

    def landed(dst, recv):
        pltpu.make_async_copy(dst, dst, recv_sems.at[recv]).wait()

    barrier = pltpu.get_barrier_semaphore()

    def greet(to_dp, to_node):
        pl.semaphore_signal(barrier, inc=1, device_id={"dp": to_dp, "node": to_node}, device_id_type=MESH)

    for step in range(1, 8):
        greet(dp, lax.rem(node + step, 8))
    greet(at_z(1), node)
    greet(at_z(-1), node)
    greet(pair, node)
    for step in range(1, 4):
        greet(at_side(lax.rem(side + step, 4)), node)
    def odd_half(where, origin):
        return lax.rem(lax.rem(where - where % 2 - origin + 16, 8) // 4 + where, 2)

    def last_to(block, cut):
        to_chip = lax.rem(chip + odd_half(z, node) + 2 * cut, 4)
        return node * 8 + lax.rem(x + block, 4) * 2 + low, to_chip * 2 + par

    def is_me(where):
        return jnp.logical_and(where[0] == dp, where[1] == node)

    expected = 13

    pl.semaphore_wait(barrier, expected)

    def quarter_rows(quarter):
        return pl.ds(pl.multiple_of(quarter * CUT, 16), CUT)

    def cols_of(to_node):
        return pl.ds(pl.multiple_of(to_node * WIDE, 128), WIDE)

    is_src = core == par
    fetch_recv = [fresh("recv") for _ in range(3)]
    stage_recv = [fresh("recv") for _ in range(3)]
    own_recv = [fresh("recv") for _ in range(2)]
    own_rows = quarter_rows(z // 2)
    far_steps = (2, 1, 3)
    for a, arr in enumerate((tok, cot)):
        here = jnp.logical_and(is_src, z % 2 == a)
        for step in far_steps:
            push(
                arr.at[own_rows, cols_of(at_chip(step) * 2 + 1 - core)], fetch_buf.at[step - 1],
                stage_recv[step - 1], dp, mate, when=here,
            )
        for step in far_steps:
            to_node = at_chip(step) * 2 + core
            push(
                arr.at[own_rows, cols_of(to_node)], acts_in.at[a, chip, own_rows, :],
                fetch_recv[step - 1], dp, to_node, when=here,
            )

    for a, arr in enumerate((tok, cot)):
        push(arr.at[:, cols_of(mate)], acts_in.at[a, chip], own_recv[a], dp, mate, when=is_src)

        @pl.when(is_src)
        def _(a=a, arr=arr):
            pltpu.make_async_copy(
                arr.at[:, cols_of(node)], acts_in.at[a, chip], recv_sems.at[own_recv[a]]
            ).start()

    not_src = jnp.logical_not(is_src)
    for step in far_steps:
        pl.when(not_src)(lambda step=step: landed(fetch_buf.at[step - 1], stage_recv[step - 1]))
        push(
            fetch_buf.at[step - 1], acts_in.at[z % 2, chip, own_rows, :], fetch_recv[step - 1],
            dp, at_chip(step) * 2 + core, when=not_src,
        )

    for load in loads:
        load.wait()
    eye = lax.broadcasted_iota(jnp.int32, (HID, HID), 0) == lax.broadcasted_iota(jnp.int32, (HID, HID), 1)
    for b in range(WIDE // QB):
        rows = slice(b * QB, (b + 1) * QB)
        line = pl.ds(node * (WIDE // QB) + b, 1)
        w_gu[0, rows, 0:HID] = (gate_codes[rows, :].astype(F32) * gate_scales[line, :]).astype(BF)
        w_gu[0, rows, HID:] = (up_codes[rows, :].astype(F32) * up_scales[line, :]).astype(BF)
        column = jnp.sum(jnp.where(eye, down_scales[line, :], 0.0), axis=1, keepdims=True)
        w_down[0, :, rows] = (down_codes[:, rows].astype(F32) * column).astype(BF)

    w_recv = [fresh("recv") for _ in range(2)]
    push(w_gu.at[0], w_gu.at[1], w_recv[0], pair, node)
    push(w_down.at[0], w_down.at[1], w_recv[1], pair, node)

    up_recv = [[fresh("recv") for _ in range(3)] for _ in range(3)]
    dn_recv = [[fresh("recv") for _ in range(3)] for _ in range(3)]
    far_recv = [fresh("recv") for _ in range(3)]

    def block(turn, step):
        piece = lax.rem(z + turn + 8, 8)
        return acts_in.at[piece % 2, at_chip(-step), quarter_rows(piece // 2), :]

    def relay(turn, step):
        if turn == 0:
            landed(block(0, step), fetch_recv[step - 1])
            push(block(0, step), block(0, step), up_recv[0][step - 1], at_z(1), node)
            push(block(0, step), block(0, step), dn_recv[0][step - 1], at_z(-1), node)
            return
        if turn == 4:
            landed(block(4, step), far_recv[step - 1])
            return
        here = block(-turn, step)
        landed(here, up_recv[turn - 1][step - 1])
        if turn < 3:
            push(here, here, up_recv[turn][step - 1], at_z(1), node)
        elif step != 3:
            push(here, here, far_recv[step - 1], at_z(1), node, when=None if step == 1 else core == 0)
        here = block(turn, step)
        landed(here, dn_recv[turn - 1][step - 1])
        if turn < 3:
            push(here, here, dn_recv[turn][step - 1], at_z(-1), node)
        elif step != 1:
            push(here, here, far_recv[step - 1], at_z(-1), node, when=None if step == 3 else core == 1)

    sign = 1 - 2 * (z % 2)
    quarters = [
        lax.rem(z + first * sign + 8, 8) // 2 for first in (0, -1, 2, -3)
    ]
    mate_recv = [fresh("recv") for _ in range(4)]
    sum_recv = [[fresh("recv") for _ in range(3)] for _ in range(4)]
    hid_recv = [[fresh("recv") for _ in range(3)] for _ in range(4)]
    hid_far = [[fresh("recv") for _ in range(3)] for _ in range(4)]
    ways = (1, 1 - 2 * core, -1)

    def cols(b):
        return slice(b * HID, (b + 1) * HID)

    hid_mate = [[fresh("recv") for _ in range(4)] for _ in range(4)]

    def multiply(s):
        rows = quarter_rows(quarters[s])
        tokens = acts_in[0, :, rows, :].reshape(4 * CUT, WIDE)
        grads = acts_in[1, :, rows, :].reshape(4 * CUT, WIDE)
        for part, store in ((1 - core, other), (core, mine)):
            store[s, :, :, 0 : 2 * HID] = (
                dot_nn(tokens, w_gu[part]).reshape(4, CUT, 2 * HID).astype(store.dtype)
            )
            store[s, :, :, 2 * HID :] = (
                dot_nt(grads, w_down[part]).reshape(4, CUT, HID).astype(store.dtype)
            )
            if store is other:
                push(other.at[s], mate_in.at[s], mate_recv[s], dp, mate)

    def combine(s):
        landed(mate_in.at[s], mate_recv[s])
        for step in far_steps:
            to = at_chip(step)
            total = mine[s, to] + mate_in[s, to]
            high = total.astype(BF)
            sum_out[s, step - 1, :, 0 : 3 * HID] = high
            sum_out[s, step - 1, :, 3 * HID :] = (total[:, 0:HID] - high[:, 0:HID].astype(F32)).astype(BF)
            push(
                sum_out.at[s, step - 1], sum_in.at[s, step - 1], sum_recv[s][step - 1],
                dp, to * 2 + core,
            )

    def activate(s):
        full = mine[s, chip] + mate_in[s, chip]
        rest = jnp.zeros((CUT, HID), F32)
        for i in (0, 2, 1):
            landed(sum_in.at[s, i], sum_recv[s][i])
            full = full + sum_in[s, i, :, 0 : 3 * HID].astype(F32)
            rest = rest + sum_in[s, i, :, 3 * HID :].astype(F32)
        rows = quarter_rows(quarters[s])
        gate, upper, d_act = full[:, 0:HID] + rest, full[:, HID : 2 * HID], full[:, 2 * HID :]
        sig = jax.nn.sigmoid(gate)
        silu = gate * sig
        hidden[core, chip, rows, 0:HID] = (d_act * upper * sig * (1.0 + gate * (1.0 - sig))).astype(BF)
        hidden[core, chip, rows, HID : 2 * HID] = (d_act * silu).astype(BF)
        hidden[core, chip, rows, 2 * HID :] = (silu * upper).astype(BF)
        own = hidden.at[core, chip, rows]
        for step in (1, 3) if s in RELAYED else far_steps:
            push(own, own, hid_recv[s][step - 1], dp, at_chip(step) * 2 + core)
        push(own, own, hid_mate[s][0], dp, mate)

    def forward_hidden(s):
        rows = quarter_rows(quarters[s])
        for step in (1, 3) if s in RELAYED else (1, 3, 2):
            here = hidden.at[core, at_chip(-step), rows]
            landed(here, hid_recv[s][step - 1])
            if s not in RELAYED:
                push(here, here, hid_mate[s][step], dp, mate)
        if s in RELAYED:
            for b in range(3):
                here = hidden.at[core, at_chip(-ways[b]), rows, cols(b)]
                push(here, here, hid_far[s][b], dp, at_chip(ways[b]) * 2 + core)
            for step in (1, 3):
                here = hidden.at[core, at_chip(-step), rows]
                push(here, here, hid_mate[s][step], dp, mate)

    def last_hidden(s):
        rows = quarter_rows(quarters[s])
        for b in range(3):
            landed(hidden.at[core, at_chip(2), rows, cols(b)], hid_far[s][b])
        here = hidden.at[core, at_chip(2), rows]
        push(here, here, hid_mate[s][2], dp, mate)

    def finish_hidden(s):
        rows = quarter_rows(quarters[s])
        for step in range(4):
            landed(hidden.at[1 - core, at_chip(-step), rows], hid_mate[s][step])

    ring_slot = {-3: 0, 3: 1, -2: 2, 2: 3, -1: 4, 1: 5, 0: 6}
    ring_recv = [[fresh("recv") for _ in range(2)] for _ in range(8)]
    buf_slot = {4: 0, 3: 1, -3: 2, 2: 3, -2: 4, 1: 5, -1: 6}
    pairs = ((4, -3), (2, 3), (-2, -1), (0, 1))

    def cut_rows(cut):
        return slice(cut * CUT, (cut + 1) * CUT)

    def token_terms(s, i):
        rows = quarter_rows(quarters[s])
        half = odd_half(lax.rem(2 * quarters[s] + 4, 8) + lax.rem(i + z, 2), node)
        total = None
        for part in range(2):
            data = jnp.concatenate(
                [hidden[part, lax.rem(chip + half + 2 * cut, 4), rows, 0 : 2 * HID] for cut in range(2)], axis=0
            )
            term = dot_nt(data, w_gu[part])
            total = term if total is None else total + term
        return total

    def chain(far):
        s, i = [(s, pair.index(far)) for s, pair in enumerate(pairs) if far in pair][0]
        terms = token_terms(s, i)
        if far == 0:
            return terms
        way = 1 if far > 0 else -1
        buf = buf_slot[far]
        for cut in range(2):
            rows = cut_rows(cut)
            value = terms[rows]
            if abs(far) < 3 or far == (-3, 3)[cut]:
                slot = ring_slot[far]
                landed(ring_in.at[slot, rows], ring_recv[slot][cut])
                value = value + ring_in[slot, rows].astype(F32)
            ring_buf[buf, rows] = value.astype(BF)
            if far == 4:
                to, slot = sign * (1 - 2 * cut), (0, 1)[cut]
            else:
                to, slot = sign * way, 7 if far == -1 else ring_slot[-(far - way)]
            push(ring_buf.at[buf, rows], ring_in.at[slot, rows], ring_recv[slot][cut], at_z(to), node)
        return None

    for step in (1, 3, 2):
        relay(0, step)
    relay(1, 1)
    relay(1, 3)
    for a in range(2):
        landed(acts_in.at[a, chip], own_recv[a])
    relay(1, 2)
    landed(w_gu.at[1], w_recv[0])
    landed(w_down.at[1], w_recv[1])
    multiply(0)
    relay(2, 1)
    combine(0)
    relay(2, 3)
    relay(2, 2)
    multiply(1)
    relay(3, 1)
    combine(1)
    relay(3, 3)
    relay(3, 2)
    multiply(2)
    activate(0)
    relay(4, 1)
    combine(2)
    relay(4, 3)
    relay(4, 2)
    multiply(3)
    activate(1)
    combine(3)
    forward_hidden(0)
    activate(2)
    forward_hidden(1)
    last_hidden(0)
    activate(3)
    finish_hidden(0)
    chain(4)
    forward_hidden(2)
    last_hidden(1)
    finish_hidden(1)
    chain(-3)
    chain(3)
    last_hidden(2)
    forward_hidden(3)
    finish_hidden(2)
    last_hidden(3)
    chain(2)
    chain(-2)
    finish_hidden(3)
    chain(-1)
    chain(1)

    def weight_grads(part):
        tokens = acts_in[0].reshape(4 * ROWS, WIDE)
        grads = acts_in[1].reshape(4 * ROWS, WIDE)
        back = hidden[part].reshape(4 * ROWS, 3 * HID)
        return dot_tn(tokens, back[:, 0 : 2 * HID]), dot_tn(back[:, 2 * HID :], grads)

    first, second = weight_grads(1)
    grad_out[...] = first.astype(BF)
    down_out[...] = second.astype(BF)
    grad_recv = [fresh("recv") for _ in range(3)]
    push(down_out, down_in, grad_recv[0], pair, node)

    terms = chain(0)

    first, second = weight_grads(0)
    grad_own[...] = first
    down_own[...] = second

    for slot in (7, 6):
        for cut in range(2):
            landed(ring_in.at[slot, cut_rows(cut)], ring_recv[slot][cut])
    terms = terms + ring_in[6].astype(F32) + ring_in[7].astype(F32)
    for i in range(8):
        turn = lax.rem(i // 2 - par + 4, 4)
        member, b = (turn // 2) * 2 + i % 2, lax.rem(turn, 2)
        side_buf[member, b, :, 0:N_COLS] = terms[:, i * N_COLS : (i + 1) * N_COLS].astype(BF)
        side_buf[member, b, :, N_COLS:] = jnp.zeros((96, 128 - N_COLS), BF)

    side_recv = [fresh("recv") for _ in range(3)]
    for step in range(1, 4):
        to = lax.rem(side + step, 4)
        push(side_buf.at[to], side_in.at[step - 1], side_recv[step - 1], at_side(to), node)
    for b in range(2):
        push(grad_out.at[:, cols(b)], grad_in.at[:, cols(b)], grad_recv[1 + b], pair, node)
    total = side_buf[side].astype(F32)
    for step in range(1, 4):
        landed(side_in.at[step - 1], side_recv[step - 1])
        total = total + side_in[step - 1].astype(F32)
    last_buf[...] = total.astype(BF)

    last_recv = fresh("recv", 4)
    quarter = lax.rem(z // 2 + 2, 4)
    for b in range(2):
        for cut in range(2):
            where = last_to(b, cut)
            src, dst, recv = last_buf.at[b, cut_rows(cut)], last_in.at[quarter], last_recv + quarter
            push(src, dst, recv, *where, when=jnp.logical_not(is_me(where)))

            @pl.when(is_me(where))
            def _(src=src, dst=dst, recv=recv):
                pltpu.make_async_copy(src, dst, recv_sems.at[recv]).start()

    landed(down_in, grad_recv[0])
    for b in range(2):
        landed(grad_in.at[:, cols(b)], grad_recv[1 + b])
    gate_grad[...] = (grad_own[:, 0:HID] + grad_in[:, 0:HID].astype(F32)).astype(BF)
    up_grad[...] = (grad_own[:, HID:] + grad_in[:, HID:].astype(F32)).astype(BF)
    down_grad[...] = (down_own[...] + down_in[...].astype(F32)).astype(BF)
    stores = [
        pltpu.make_async_copy(src, dst, store_sems.at[i])
        for i, (src, dst) in enumerate((
            (gate_grad, gate_grad_hbm), (up_grad, up_grad_hbm), (down_grad, down_grad_hbm),
            (token_grad, token_grad_hbm),
        ))
    ]
    for store in stores[:3]:
        store.start()

    for i in range(4):
        landed(last_in.at[i], last_recv + i)
    token_grad[...] = jnp.transpose(last_in[...].reshape(ROWS, 128).astype(F32))[0:N_COLS, :].astype(BF)
    stores[3].start()

    assert max(counts.values()) <= SEMS

    for copy, when in sent:
        if when is None:
            copy.wait_send()
        else:
            pl.when(when)(copy.wait_send)
    for store in stores:
        store.wait()


def write_out(*refs):
    for src, dst in zip(refs[:4], refs[4:]):
        dst[...] = src[...]


def body(tok, cot, gate_codes, up_codes, down_codes, gate_scales, up_scales, down_scales):
    hbm = pl.BlockSpec(memory_space=pltpu.HBM)
    outs = (
        jax.ShapeDtypeStruct((N_COLS, ROWS), BF),
        jax.ShapeDtypeStruct((WIDE, HID), BF),
        jax.ShapeDtypeStruct((WIDE, HID), BF),
        jax.ShapeDtypeStruct((HID, WIDE), BF),
    )
    results = pl.pallas_call(
        kernel,
        out_shape=outs,
        in_specs=[hbm] * 8,
        out_specs=(hbm,) * 4,
        scratch_shapes=[
            pltpu.VMEM((N_COLS, ROWS), BF),
            pltpu.VMEM((WIDE, HID), BF),
            pltpu.VMEM((WIDE, HID), BF),
            pltpu.VMEM((HID, WIDE), BF),
            pltpu.VMEM((WIDE, HID), BF),
            pltpu.VMEM((WIDE, HID), BF),
            pltpu.VMEM((HID, WIDE), BF),
            pltpu.VMEM((40, HID), F32),
            pltpu.VMEM((40, HID), F32),
            pltpu.VMEM((40, HID), F32),
            pltpu.VMEM((2, 4, ROWS, WIDE), BF),
            pltpu.VMEM((3, CUT, WIDE), BF),
            pltpu.VMEM((2, WIDE, 2 * HID), BF),
            pltpu.VMEM((2, HID, WIDE), BF),
            pltpu.VMEM((4, 4, CUT, 3 * HID), F32),
            pltpu.VMEM((4, 4, CUT, 3 * HID), F32),
            pltpu.VMEM((4, 4, CUT, 3 * HID), F32),
            pltpu.VMEM((4, 3, CUT, 4 * HID), BF),
            pltpu.VMEM((4, 3, CUT, 4 * HID), BF),
            pltpu.VMEM((2, 4, ROWS, 3 * HID), BF),
            pltpu.VMEM((WIDE, 2 * HID), BF),
            pltpu.VMEM((HID, WIDE), BF),
            pltpu.VMEM((WIDE, 2 * HID), BF),
            pltpu.VMEM((HID, WIDE), BF),
            pltpu.VMEM((WIDE, 2 * HID), F32),
            pltpu.VMEM((HID, WIDE), F32),
            pltpu.VMEM((7, 96, WIDE), BF),
            pltpu.VMEM((8, 96, WIDE), BF),
            pltpu.VMEM((4, 2, 96, 128), BF),
            pltpu.VMEM((3, 2, 96, 128), BF),
            pltpu.VMEM((2, 96, 128), BF),
            pltpu.VMEM((4, CUT, 128), BF),
            pltpu.SemaphoreType.DMA((6,)),
            pltpu.SemaphoreType.DMA((4,)),
            pltpu.SemaphoreType.DMA((SEMS,)),
            pltpu.SemaphoreType.DMA((SEMS,)),
        ],
        compiler_params=pltpu.CompilerParams(
            collective_id=0, has_side_effects=True, vmem_limit_bytes=VMEM_BYTES
        ),
        cost_estimate=pl.CostEstimate(flops=2_100_000_000, bytes_accessed=5_000_000, transcendentals=25_000),
    )(tok, cot, gate_codes, up_codes, down_codes, gate_scales, up_scales, down_scales.T)
    results = pl.pallas_call(
        write_out,
        out_shape=outs,
        compiler_params=pltpu.CompilerParams(vmem_limit_bytes=VMEM_BYTES),
    )(*results)
    return (results[0].T,) + tuple(results[1:])


def solution(mesh):
    return jax.shard_map(
        body,
        mesh=mesh,
        in_specs=(
            P("node", None),
            P("node", None),
            P("node", "dp"),
            P("node", "dp"),
            P("dp", "node"),
            P(None, "dp"),
            P(None, "dp"),
            P("dp", None),
        ),
        out_specs=(P("node", "dp"), P("node", "dp"), P("node", "dp"), P("dp", "node")),
        check_vma=False,
    )
```
